128 devices in a mesh: fsdp: 8 (over x, core), ctx: 2 (over y_lo), tp: 8 (over y_hi, z).
Axes of the slice: x: 4, y: 4 (y_hi: 2, y_lo: 2; y = y_hi * 2 + y_lo), z: 4, core: 2. Of those that a mesh axis runs over, the one named last changes fastest.
Arguments:
- tokens: bfloat16 [16384, 1024], P(('fsdp', 'ctx', 'tp')), may hold values from -6 to 6
- lengths: int32 [8, 1], P('fsdp'), may hold values from 1026 to 2048, as said below
- gain_one: float32 [1024], replicated, may hold values from 0.5 to 1.5
- w_in: bfloat16 [1024, 3, 1024], P(('fsdp', 'ctx'), None, 'tp'), may hold values from -0.1875 to 0.1875
- conv_weight: float32 [3, 1024], replicated, may hold values from -3.5 to 3.5
- w_out: bfloat16 [1024, 1024], P('tp', ('fsdp', 'ctx')), may hold values from -0.1875 to 0.1875
- gain_two: float32 [1024], replicated, may hold values from 0.5 to 1.5
- w_gu: bfloat16 [2, 1024, 4608], P(None, ('fsdp', 'ctx'), 'tp'), may hold values from -0.1875 to 0.1875
- w_down: bfloat16 [4608, 1024], P('tp', ('fsdp', 'ctx')), may hold values from -0.1875 to 0.1875
- cotangent: bfloat16 [16384, 1024], P(('fsdp', 'ctx', 'tp')), may hold values from -24 to 24
Outputs:
- mixed: bfloat16 [16384, 1024], P(('fsdp', 'ctx', 'tp'))
- grad_tokens: float32 [16384, 1024], P(('fsdp', 'ctx', 'tp'))
- grad_gain_one: float32 [1024], replicated
- grad_w_in: float32 [1024, 3, 1024], P(('fsdp', 'ctx'), None, 'tp')
- grad_conv: float32 [3, 1024], replicated
- grad_w_out: float32 [1024, 1024], P('tp', ('fsdp', 'ctx'))
- grad_gain_two: float32 [1024], replicated
- grad_w_gu: float32 [2, 1024, 4608], P(None, ('fsdp', 'ctx'), 'tp')
- grad_w_down: float32 [4608, 1024], P('tp', ('fsdp', 'ctx'))
The draws below stay inside these ranges and needn't reach their ends.
Inputs may be any that keep to these rules, and one draw needn't show every extreme that they name: `lengths`: row g holds the length of the one sequence that begins at the first token of group g; the token slots after it are padding; some group's sequence fills all 2048 slots.
All inputs are finite; a program needn't handle non-finite values.
Results may differ from the reference program's by a relative error of at most 0.025.
Values may be sent and summed in bfloat16 or wider, within the bound.
No kernel may reach another device: no remote copies, remote signals or barrier semaphores. Data moves between devices by JAX's collectives and lax.ppermute only.
A program may use at most 128 MiB of HBM per device.

```python
import jax
import jax.numpy as jnp
from jax import lax

D = 1024
FF = 4608
SEQ_TOK = 2048
NSEQ = 1
GROUPS = 8
TOKENS = 16384
N_FSDP = 8


def draw_lengths(key, part):
    key = jax.random.fold_in(key, 11)
    key_len, key_full = jax.random.split(key)
    drawn = jax.random.randint(key_len, (GROUPS, NSEQ), SEQ_TOK // 2 + 2, SEQ_TOK + 1, dtype=jnp.int32)
    full_row = jax.random.randint(key_full, (), 0, GROUPS, dtype=jnp.int32)
    rows = jnp.arange(GROUPS, dtype=jnp.int32)[:, None]
    return jnp.where(rows == full_row, jnp.int32(SEQ_TOK), drawn).astype(jnp.int32)


def strengthened(array, own_key, source, target, parts, factor):
    owner, partner = [(jnp.arange(array.shape[axis_at]) // (array.shape[axis_at] // parts)).reshape([-1 if axis == axis_at else 1 for axis in range(array.ndim)]) for axis_at in (source, target)]
    chosen = jax.random.permutation(own_key, parts)[partner]
    strong = (owner == chosen) | (owner == (partner + parts // 2) % parts)
    return jnp.where(strong, factor * array, array)


def shard_levels(key, dims, cuts, low, top_value):
    loudness = 1.0
    for dim, blocks in cuts:
        steps = jax.random.uniform(jax.random.fold_in(jax.random.fold_in(key, 6), dim), (blocks,), jnp.float32, low / len(cuts), top_value / len(cuts))
        loudness = loudness * jnp.repeat(jnp.exp(steps), dims[dim] // blocks).reshape((-1,) + (1,) * (len(dims) - 1 - dim))
    return loudness


def gaussian(stream_key, shape, deviation, reach, cuts=(), held_as=jnp.bfloat16):
    factor_of = shard_levels(stream_key, shape, cuts, -0.22, 0.18) if cuts else 1.0
    values = jax.random.normal(stream_key, shape, jnp.float32) * deviation * factor_of
    return jnp.minimum(jnp.maximum(values, -reach), reach).astype(held_as)


def bell_draw_with(key, shape, deviation, most, cuts, heavy, held_as=jnp.bfloat16):
    array = deviation * jax.random.normal(key, shape, jnp.float32)
    if cuts:
        array = array * shard_levels(key, shape, cuts, -0.22, 0.18)
    return jnp.clip(strengthened(array, jax.random.fold_in(key, 3), *heavy), -most, most).astype(held_as)


def setup_inputs(seed: int = 0) -> dict:
    key_of = jax.random.split(jax.random.key(seed), 11)
    return {
        "tokens": gaussian(key_of[0], (TOKENS, D), 1.0, 6.0, ((0, 128),)),
        "lengths": draw_lengths(jax.random.fold_in(key_of[10], 71), 0),
        "gain_one": jnp.clip(1.0 + 0.1 * jax.random.normal(key_of[2], (D,), jnp.float32), 0.5, 1.5),
        "w_in": gaussian(key_of[3], (D, 3, D), D ** -0.5, 0.1875, ((0, 16), (2, 8))),
        "conv_weight": gaussian(key_of[4], (3, D), 3 ** -0.5, 3.5, (), jnp.float32),
        "w_out": gaussian(key_of[5], (D, D), D ** -0.5, 0.1875, ((0, 8), (1, 16))),
        "gain_two": jnp.clip(1.0 + 0.1 * jax.random.normal(key_of[6], (D,), jnp.float32), 0.5, 1.5),
        "w_gu": gaussian(key_of[7], (2, D, FF), D ** -0.5, 0.1875, ((1, 16), (2, 8))),
        "w_down": gaussian(key_of[8], (FF, D), (FF // 4) ** -0.5, 0.1875, ((0, 8), (1, 16))),
        "cotangent": bell_draw_with(key_of[9], (TOKENS, D), 1.0, 24.0, ((0, 128),), (0, 1, 128, 5.5)),
    }


EPS = 1e-05
PRECISE = lax.Precision.HIGHEST

@jax.custom_vjp
def low(v):
    return lax.optimization_barrier(v.astype(jnp.bfloat16)).astype(jnp.float32)

@jax.custom_vjp
def low_back(v):
    return v

def low_keep(v):
    return (low(v), None)

def low_pass(kept, grad):
    return (grad,)

def back_keep(v):
    return (v, None)

def back_low(kept, grad):
    return (low(grad),)
low.defvjp(low_keep, low_pass)
low_back.defvjp(back_keep, back_low)

def rms_scale(values):
    return lax.rsqrt(lax.optimization_barrier(jnp.mean(values * values, axis=-1, keepdims=True)) + EPS)

def segment_links(lengths_row):
    seq_ends = jnp.cumsum(lengths_row).astype(jnp.int32)
    places = jnp.arange(SEQ_TOK, dtype=jnp.int32)
    live = places < seq_ends[-1]
    segment = lax.optimization_barrier(jnp.sum((places[:, None] >= seq_ends[None, :]).astype(jnp.int32), axis=1)).astype(jnp.int32)
    same_one = ((segment[1:] == segment[:-1]) & live[1:] & live[:-1]).astype(jnp.float32)
    same_two = ((segment[2:] == segment[:-2]) & live[2:] & live[:-2]).astype(jnp.float32)
    link_one = jnp.concatenate([jnp.zeros((1,), jnp.float32), same_one])[:, None]
    link_two = jnp.concatenate([jnp.zeros((2,), jnp.float32), same_two])[:, None]
    return (link_one, link_two)

def block_forward(tokens_f, param_list, link_one, link_two):
    gain_one, w_in, conv_weight, w_out, gain_two, w_gu, w_down = param_list
    normed_one = low(tokens_f * rms_scale(tokens_f) * gain_one)
    projected = low_back(jnp.einsum('td,dkc->tkc', normed_one, w_in, precision=PRECISE))
    b_values = projected[:, 0]
    c_values = projected[:, 1]
    x_values = projected[:, 2]
    product = low(b_values * x_values)
    width = product.shape[1]
    before_one = jnp.concatenate([jnp.zeros((1, width), jnp.float32), product[:-1]], axis=0)
    before_two = jnp.concatenate([jnp.zeros((2, width), jnp.float32), product[:-2]], axis=0)
    conv_out = low_back(conv_weight[2] * product + link_one * conv_weight[1] * before_one + link_two * conv_weight[0] * before_two)
    gated = low(c_values * conv_out)
    mixer = low_back(jnp.dot(gated, w_out, precision=PRECISE))
    middle = tokens_f + mixer
    normed_two = low(middle * rms_scale(middle) * gain_two)
    gate_up = low_back(jnp.einsum('td,kdf->tkf', normed_two, w_gu, precision=PRECISE))
    activation = low(jax.nn.silu(gate_up[:, 0]) * gate_up[:, 1])
    return middle + jnp.dot(activation, w_down, precision=PRECISE)

def combine_sum(existing, update):
    return existing + update

def reference(tokens, lengths, gain_one, w_in, conv_weight, w_out, gain_two, w_gu, w_down, cotangent):
    params = tuple((item.astype(jnp.float32) for item in (gain_one, w_in, conv_weight, w_out, gain_two, w_gu, w_down)))
    token_groups = tokens.astype(jnp.float32).reshape(N_FSDP, SEQ_TOK, D)
    cot_groups = cotangent.astype(jnp.float32).reshape(N_FSDP, SEQ_TOK, D)

    def group_step(running, inputs):
        tokens_group, cot_group, lengths_row = inputs
        link_one, link_two = segment_links(lengths_row)

        def forward(tokens_f, param_list):
            return block_forward(tokens_f, param_list, link_one, link_two)
        result, pullback = jax.vjp(forward, tokens_group, params)
        grad_group, grad_params = pullback(cot_group)
        running = jax.tree.map(combine_sum, running, grad_params)
        return (running, (result.astype(jnp.bfloat16), grad_group))
    initial = tuple((jnp.zeros_like(item) for item in params))
    totals, (results, grad_groups) = lax.scan(group_step, initial, (token_groups, cot_groups, lengths))
    mixed = results.reshape(TOKENS, D)
    grad_tokens = grad_groups.reshape(TOKENS, D)
    g_one, g_in, g_conv, g_out, g_two, g_gu, g_down = totals
    return (mixed, grad_tokens, g_one, g_in, g_conv, g_out, g_two, g_gu, g_down)
```

```python
import jax
import jax.numpy as jnp
from jax import lax
from jax.experimental import pallas as pl
from jax.experimental.pallas import tpu as pltpu
from jax.sharding import Mesh
from jax.sharding import PartitionSpec as P

EPS = 1e-05
F32 = jnp.float32
BF16 = jnp.bfloat16
AXES = ("x", "core", "ylo", "yhi", "z")
SIZES = (4, 2, 2, 2, 4)
CONTRACT_LAST = (((1,), (1,)), ((), ()))
CONTRACT_FIRST = (((0,), (0,)), ((), ()))
FF_BLOCK = 576
FF_PAD = 640


def device_number(x, core, y, z):
    return (((x * 2 + core) * 2 + y % 2) * 2 + y // 2) * 4 + z


def route(step):
    return [
        (device_number(x, core, y, z), device_number(*step(x, core, y, z)))
        for x in range(4)
        for core in range(2)
        for y in range(4)
        for z in range(4)
    ]


def along_z(value, m):
    return lax.ppermute(value, AXES, route(lambda x, c, y, z: (x, c, y, z ^ m)))


def along_x(value, m):
    return lax.ppermute(value, AXES, route(lambda x, c, y, z: (x ^ m, c, y, z)))


def along_y(value, m):
    return lax.ppermute(value, AXES, route(lambda x, c, y, z: (x, c, y ^ m, z)))


def other_core(value):
    return lax.ppermute(value, AXES, route(lambda x, c, y, z: (x, 1 - c, y, z)))


def first_axis(value, m):
    def step(x, c, y, z):
        return (x ^ m, c, y, z) if c == 0 else (x, c, y ^ m, z)

    return lax.ppermute(value, AXES, route(step))


def second_axis(value, m):
    def step(x, c, y, z):
        return (x, c, y ^ m, z) if c == 0 else (x ^ m, c, y, z)

    return lax.ppermute(value, AXES, route(step))


def all_z(own):
    got = {m: along_z(own, m) for m in (2, 1, 3)}
    return jnp.concatenate([own, got[1], got[2], got[3]], axis=0)


def sum_z(blocks):
    got = {m: along_z(blocks[m], m) for m in (2, 1, 3)}
    return (
        blocks[0].astype(F32) + got[1].astype(F32) + got[2].astype(F32) + got[3].astype(F32)
    )


def gather_plane(pack):
    got = {m: first_axis(pack, m) for m in (2, 1, 3)}
    first = jnp.stack([pack, got[1], got[2], got[3]])
    mine = {m: second_axis(first, m) for m in (2, 1, 3)}
    mine[0] = first
    theirs = {m: other_core(mine[m]) for m in (0, 1, 3, 2)}
    return [mine[m] for m in range(4)] + [theirs[m] for m in range(4)]


def place_kernel(count, split, block, *refs):
    pieces, outs, sems = refs[:8], refs[8:10], refs[10]
    x = lax.axis_index("x")
    core = lax.axis_index("core")
    y = lax.axis_index("yhi") * 2 + lax.axis_index("ylo")
    copies = []
    for p in range(8):
        k = core if p < 4 else 1 - core
        for m in range(4):
            x_from = jnp.where(k == 0, x ^ m, x ^ (p % 4))
            y_from = jnp.where(k == 0, y ^ (p % 4), y ^ m)
            row = pl.multiple_of(((x_from * 2 + k) * 2 + y_from % 2) * 64, 64)
            for i in range(count):
                out, at = (outs[0], i) if i < split else (outs[1], i - split)
                col = pl.multiple_of((at * 2 + y_from // 2) * block, 128)
                copies.append(
                    pltpu.make_async_copy(
                        pieces[p].at[m, i],
                        out.at[pl.ds(row, 64), pl.ds(col, block)],
                        sems.at[len(copies)],
                    )
                )
    for c in copies:
        c.start()
    for c in copies:
        c.wait()


def placed(pieces, split):
    _, count, _, block = pieces[0].shape

    def kernel(*refs):
        place_kernel(count, split, block, *refs)

    return pl.pallas_call(
        kernel,
        out_shape=(
            jax.ShapeDtypeStruct((1024, split * 2 * block), BF16),
            jax.ShapeDtypeStruct((1024, (count - split) * 2 * block), BF16),
        ),
        in_specs=[pl.BlockSpec(memory_space=pl.ANY)] * 8,
        out_specs=(pl.BlockSpec(memory_space=pltpu.VMEM), pl.BlockSpec(memory_space=pltpu.VMEM)),
        scratch_shapes=[pltpu.SemaphoreType.DMA((32 * count,))],
        cost_estimate=pl.CostEstimate(
            flops=0, bytes_accessed=2 * 2 * 32 * count * 64 * block, transcendentals=0
        ),
        compiler_params=pltpu.CompilerParams(vmem_limit_bytes=40 * 2**20),
    )(*pieces)


def core_columns(value, core):
    rows = value.shape[0]
    return lax.dynamic_slice_in_dim(value.reshape(rows, 4, 2, 128), core, 1, 2).reshape(rows, 512)


def scatter_plane(pairs, core, x, y, block):
    parts = []
    for left, right in pairs:
        sent = lax.dot_general(
            core_columns(left, 1 - core), right, CONTRACT_FIRST, preferred_element_type=F32
        ).astype(BF16)
        kept = lax.dot_general(
            core_columns(left, core), right, CONTRACT_FIRST, preferred_element_type=F32
        )
        half = (kept + other_core(sent).astype(F32)).astype(BF16)
        parts.append(half.reshape(4, 2, 64, -1, 2, block))

    def slice_for(m):
        y_to = y ^ m
        x_to = x ^ m
        out = []
        for part in parts:
            by_y = lax.dynamic_slice_in_dim(part, y_to % 2, 1, 1)
            by_y = lax.dynamic_slice_in_dim(by_y, y_to // 2, 1, 4)[:, 0, :, :, 0, :]
            by_x = lax.dynamic_slice_in_dim(part, x_to, 1, 0)[0]
            by_x = by_x.transpose(3, 0, 1, 2, 4).reshape(by_y.shape)
            out.append(jnp.where(core == 0, by_y, by_x))
        return jnp.concatenate(out, axis=2)

    got = {m: second_axis(slice_for(m), m) for m in (2, 1, 3)}
    quarter = (
        slice_for(0).astype(F32) + got[1].astype(F32) + got[2].astype(F32) + got[3].astype(F32)
    ).astype(BF16)
    place = jnp.where(core == 0, x, y)
    pick = lambda m: lax.dynamic_index_in_dim(quarter, place ^ m, 0, keepdims=False)
    last = {m: first_axis(pick(m), m) for m in (2, 1, 3)}
    return pick(0).astype(F32) + last[1].astype(F32) + last[2].astype(F32) + last[3].astype(F32)


def sum_everywhere(vector):
    vector = vector + other_core(vector)
    for step in (along_x, along_y, along_z):
        vector = vector + step(vector, 1) + step(vector, 3) + step(vector, 2)
    return vector


def neighbour_rows(rows, outside, z, offset):
    candidates = jnp.concatenate([rows, outside[None]], axis=0)
    m = jnp.arange(4)
    target = (z ^ m) + offset
    index = jnp.where((target >= 0) & (target < 4), target ^ z, 4)
    chosen = index[:, None] == jnp.arange(5)[None, :]
    return jnp.sum(
        jnp.where(chosen[:, :, None, None], candidates[None].astype(F32), 0.0), axis=1
    )


def body(tokens, lengths, gain_one, w_in, conv_weight, w_out, gain_two, w_gu, w_down, cotangent):
    x = lax.axis_index("x")
    core = lax.axis_index("core")
    ylo = lax.axis_index("ylo")
    yhi = lax.axis_index("yhi")
    z = lax.axis_index("z")
    y = yhi * 2 + ylo
    group = ylo * 2 + yhi

    mixer_pack = jnp.concatenate([w_in.transpose(1, 0, 2), w_out.T[None]], axis=0)
    ffn_pack = jnp.pad(
        jnp.concatenate([w_gu, w_down.T[None]], axis=0), ((0, 0), (0, 0), (0, FF_PAD - FF_BLOCK))
    )
    tokens_all = all_z(tokens)
    win, wout = placed(gather_plane(mixer_pack), 3)
    cot_all = all_z(cotangent)
    wgu, wdown = placed(gather_plane(ffn_pack), 2)

    residual = tokens.astype(F32)
    values = tokens_all.astype(F32)
    scale_one = lax.rsqrt(jnp.mean(values * values, axis=-1, keepdims=True) + EPS)
    normed_one = (values * scale_one * gain_one).astype(BF16)

    projected = jnp.dot(normed_one, win, preferred_element_type=F32)
    b_values = projected[:, :256].reshape(4, 128, 256)
    c_values = projected[:, 256:512].reshape(4, 128, 256)
    x_values = projected[:, 512:].reshape(4, 128, 256)
    product = (b_values * x_values).astype(BF16)

    length = lengths[0, 0]
    start = (group * 4 + (z ^ jnp.arange(4))) * 128
    places = (start[:, None] + jnp.arange(128)[None, :])[:, :, None]
    one_fwd = ((places >= 1) & (places < length)).astype(F32)
    two_fwd = ((places >= 2) & (places < length)).astype(F32)
    one_back = (places + 1 < length).astype(F32)
    two_back = (places + 2 < length).astype(F32)
    taps = jnp.concatenate(
        [
            lax.dynamic_slice_in_dim(conv_weight, z * 128, 128, 1),
            lax.dynamic_slice_in_dim(conv_weight, 512 + z * 128, 128, 1),
        ],
        axis=1,
    )

    ends = product[:, 126:]
    sent_end = lax.dynamic_index_in_dim(ends, 3 ^ z, 0, keepdims=False)
    outside = lax.ppermute(sent_end, ("ylo", "yhi"), [(0, 1), (1, 2), (2, 3)])
    before = neighbour_rows(ends, outside, z, -1)
    extended = jnp.concatenate([before, product.astype(F32)], axis=1)
    conv_out = (
        taps[2] * extended[:, 2:]
        + one_fwd * taps[1] * extended[:, 1:-1]
        + two_fwd * taps[0] * extended[:, :-2]
    )
    gated = (c_values * conv_out).astype(BF16).reshape(512, 256)
    mixer_part = lax.dot_general(gated, wout, CONTRACT_LAST, preferred_element_type=F32)
    mixer = sum_z(mixer_part.astype(BF16).reshape(4, 128, 1024))
    middle = residual + mixer
    scale_two = lax.rsqrt(jnp.mean(middle * middle, axis=-1, keepdims=True) + EPS)
    unit_two = middle * scale_two
    normed_two = all_z((unit_two * gain_two).astype(BF16))

    gate_up = jnp.dot(normed_two, wgu, preferred_element_type=F32)
    gate_pre = gate_up[:, : 2 * FF_PAD]
    upward = gate_up[:, 2 * FF_PAD :]
    d_act = jnp.dot(cot_all, wdown, preferred_element_type=F32)
    sig = jax.nn.sigmoid(gate_pre)
    swish = gate_pre * sig
    activation = (swish * upward).astype(BF16)
    d_gate = (d_act * upward * sig * (1.0 + gate_pre * (1.0 - sig))).astype(BF16)
    d_up = (d_act * swish).astype(BF16)
    d_gu = jnp.concatenate([d_gate, d_up], axis=1)
    d_two_part = lax.dot_general(d_gu, wgu, CONTRACT_LAST, preferred_element_type=F32)
    d_normed_two = sum_z(d_two_part.astype(BF16).reshape(4, 128, 1024))
    pulled = d_normed_two * gain_two
    d_middle = cotangent.astype(F32) + scale_two * (
        pulled - unit_two * jnp.mean(pulled * unit_two, axis=-1, keepdims=True)
    )
    gain_two_part = jnp.sum(d_normed_two * unit_two, axis=0)
    d_mixer = all_z(d_middle.astype(BF16))

    ffn_part = lax.dot_general(activation, wdown, CONTRACT_LAST, preferred_element_type=F32)
    ffn_out = sum_z(ffn_part.astype(BF16).reshape(4, 128, 1024))
    mixed = (middle + ffn_out).astype(BF16)
    ffn_grads = scatter_plane([(normed_two, d_gu), (cot_all, activation)], core, x, y, FF_PAD)

    d_gated = jnp.dot(d_mixer, wout, preferred_element_type=F32).reshape(4, 128, 256)
    d_cvals = d_gated * conv_out
    d_conv = (d_gated * c_values).astype(BF16)
    starts = d_conv[:, :2]
    sent_start = lax.dynamic_index_in_dim(starts, z, 0, keepdims=False)
    outside_back = lax.ppermute(sent_start, ("ylo", "yhi"), [(1, 0), (2, 1), (3, 2)])
    after = neighbour_rows(starts, outside_back, z, 1)
    d_full = d_conv.astype(F32)
    d_extended = jnp.concatenate([d_full, after], axis=1)
    d_product = (
        taps[2] * d_extended[:, :-2]
        + one_back * taps[1] * d_extended[:, 1:-1]
        + two_back * taps[0] * d_extended[:, 2:]
    )
    taps_part = jnp.stack(
        [
            jnp.sum(d_full * two_fwd * extended[:, :-2], axis=(0, 1)),
            jnp.sum(d_full * one_fwd * extended[:, 1:-1], axis=(0, 1)),
            jnp.sum(d_full * extended[:, 2:], axis=(0, 1)),
        ]
    )
    d_projected = (
        jnp.concatenate([d_product * x_values, d_cvals, d_product * b_values], axis=2)
        .astype(BF16)
        .reshape(512, 768)
    )
    d_one_part = lax.dot_general(d_projected, win, CONTRACT_LAST, preferred_element_type=F32)
    d_normed_one = sum_z(d_one_part.astype(BF16).reshape(4, 128, 1024))
    gain_one_part = jnp.sum(d_one_part * (values * scale_one), axis=0)
    mixer_grads = scatter_plane([(normed_one, d_projected), (d_mixer, gated)], core, x, y, 128)

    scale_own = scale_one[:128]
    unit_one = residual * scale_own
    pulled_one = d_normed_one * gain_one
    grad_tokens = d_middle + scale_own * (
        pulled_one - unit_one * jnp.mean(pulled_one * unit_one, axis=-1, keepdims=True)
    )

    spread = jnp.zeros(conv_weight.shape, F32)
    spread = lax.dynamic_update_slice_in_dim(spread, taps_part[:, :128], z * 128, 1)
    spread = lax.dynamic_update_slice_in_dim(spread, taps_part[:, 128:], 512 + z * 128, 1)
    small = jnp.concatenate([gain_one_part[None], gain_two_part[None], spread], axis=0)
    small = sum_everywhere(small)

    return (
        mixed,
        grad_tokens,
        small[0],
        mixer_grads[:, :3],
        small[2:],
        mixer_grads[:, 3].T,
        small[1],
        ffn_grads[:, :2, :FF_BLOCK].transpose(1, 0, 2),
        ffn_grads[:, 2, :FF_BLOCK].T,
    )


def solution(mesh):
    fine = Mesh(mesh.devices.reshape(SIZES), AXES)
    rows = P(AXES, None)
    fsdp_ctx = ("x", "core", "ylo")
    tp = ("yhi", "z")
    return jax.shard_map(
        body,
        mesh=fine,
        in_specs=(
            rows,
            P(("x", "core"), None),
            P(),
            P(fsdp_ctx, None, tp),
            P(),
            P(tp, fsdp_ctx),
            P(),
            P(None, fsdp_ctx, tp),
            P(tp, fsdp_ctx),
            rows,
        ),
        out_specs=(
            rows,
            rows,
            P(),
            P(fsdp_ctx, None, tp),
            P(),
            P(tp, fsdp_ctx),
            P(),
            P(None, fsdp_ctx, tp),
            P(tp, fsdp_ctx),
        ),
        check_vma=False,
    )
```

```python
import jax
import jax.numpy as jnp
from jax import lax
from jax.experimental import pallas as pl
from jax.experimental.pallas import tpu as pltpu
from jax.sharding import Mesh
from jax.sharding import PartitionSpec as P

EPS = 1e-05
F32 = jnp.float32
BF16 = jnp.bfloat16
AXES = ("x", "core", "ylo", "yhi", "z")
SIZES = (4, 2, 2, 2, 4)
SPACE_ANY = pl.BlockSpec(memory_space=pl.ANY)
SPACE_VMEM = pl.BlockSpec(memory_space=pltpu.VMEM)
SPACE_SMEM = pl.BlockSpec(memory_space=pltpu.SMEM)
CONTRACT_LAST = (((1,), (1,)), ((), ()))
CONTRACT_FIRST = (((0,), (0,)), ((), ()))
FF_BLOCK = 576
FF_PAD = 640


def device_number(x, core, y, z):
    return (((x * 2 + core) * 2 + y % 2) * 2 + y // 2) * 4 + z


def route(step):
    return [
        (device_number(x, core, y, z), device_number(*step(x, core, y, z)))
        for x in range(4)
        for core in range(2)
        for y in range(4)
        for z in range(4)
    ]


def along_z(value, m):
    return lax.ppermute(value, AXES, route(lambda x, c, y, z: (x, c, y, z ^ m)))


def along_x(value, m):
    return lax.ppermute(value, AXES, route(lambda x, c, y, z: (x ^ m, c, y, z)))


def along_y(value, m):
    return lax.ppermute(value, AXES, route(lambda x, c, y, z: (x, c, y ^ m, z)))


def other_core(value):
    return lax.ppermute(value, AXES, route(lambda x, c, y, z: (x, 1 - c, y, z)))


def first_axis(value, m):
    def step(x, c, y, z):
        return (x ^ m, c, y, z) if c == 0 else (x, c, y ^ m, z)

    return lax.ppermute(value, AXES, route(step))


def second_axis(value, m):
    def step(x, c, y, z):
        return (x, c, y ^ m, z) if c == 0 else (x ^ m, c, y, z)

    return lax.ppermute(value, AXES, route(step))


def second_groups():
    groups = [
        [device_number(x, 0, y, z) for y in range(4)] for x in range(4) for z in range(4)
    ]
    return groups + [
        [device_number(x, 1, y, z) for x in range(4)] for y in range(4) for z in range(4)
    ]


def grouped_second(own):
    spread = jnp.broadcast_to(own[None], (4, *own.shape))
    return lax.all_to_all(spread, AXES, 0, 0, axis_index_groups=second_groups())


def together(*values):
    return lax.optimization_barrier(values)


def all_z(own):
    got = {m: along_z(own, m) for m in (2, 1, 3)}
    return [own, got[1], got[2], got[3]]


def sum_z(blocks):
    got = {m: along_z(blocks[m], m) for m in (2, 1, 3)}
    return sum(v.astype(F32) for v in (blocks[0], got[1], got[2], got[3]))


def all_first(own):
    got = {m: first_axis(own, m) for m in (2, 1, 3)}
    return [own, got[1], got[2], got[3]]


def all_second(own):
    got = {m: second_axis(own, m) for m in (2, 1, 3)}
    return [own, got[1], got[2], got[3]]


def both_cores(pieces):
    return [*pieces, other_core(pieces[0]), other_core(jnp.stack(pieces[1:]))]


def split_rows(vector, rows, width):
    high = lax.reduce_precision(vector, 8, 7)
    both = jnp.stack([high.astype(BF16), (vector - high).astype(BF16)]).reshape(-1, width)
    return jnp.pad(both, ((0, rows - both.shape[0]), (0, 0)))


def joined_rows(rows, shape):
    count = shape[0] * shape[1] // rows.shape[1]
    return (rows[:count] + rows[count : 2 * count]).reshape(shape)


def from_group(block, shift):
    pairs = []
    for x in range(4):
        for c in range(2):
            for y in range(4):
                for z in range(4):
                    to = (y % 2) * 2 + y // 2 - shift
                    if 0 <= to < 4:
                        target = device_number(x, c, (to % 2) * 2 + to // 2, z)
                        pairs.append((device_number(x, c, y, z), target))
    return lax.ppermute(block, AXES, pairs)


def position():
    y = lax.axis_index("yhi") * 2 + lax.axis_index("ylo")
    return lax.axis_index("x"), lax.axis_index("core"), y, lax.axis_index("z")


def first_token(m):
    _, _, y, z = position()
    return (((y % 2) * 2 + y // 2) * 4 + (z ^ m)) * 128


def weight_copies(pieces, targets, sems):
    x, core, y, _ = position()
    sources = [*pieces[:5], *(pieces[5].at[i] for i in range(3))]
    copies = []
    for ref, start, count, width in targets:
        for i in range(count):
            for p in range(8):
                k = core if p < 4 else 1 - core
                for m in range(4):
                    x_from = jnp.where(k == 0, x ^ m, x ^ (p % 4))
                    y_from = jnp.where(k == 0, y ^ (p % 4), y ^ m)
                    row = pl.multiple_of(((x_from * 2 + k) * 2 + y_from % 2) * 64, 64)
                    col = pl.multiple_of((i * 2 + y_from // 2) * width, 128)
                    copies.append(
                        pltpu.make_async_copy(
                            sources[p].at[m, :, pl.ds(start + i * width, width)],
                            ref.at[pl.ds(row, 64), pl.ds(col, width)],
                            sems.at[len(copies)],
                        )
                    )
    return copies


def grouped_copies(pieces, targets, sems):
    x, core, y, _ = position()
    copies = []
    for p in range(2):
        k = core if p == 0 else 1 - core
        for s in range(4):
            for m in range(4):
                x_from = jnp.where(k == 0, x ^ m, s)
                y_from = jnp.where(k == 0, s, y ^ m)
                row = pl.multiple_of(((x_from * 2 + k) * 2 + y_from % 2) * 64, 64)
                for ref, start, count, width in targets:
                    for i in range(count):
                        col = pl.multiple_of((i * 2 + y_from // 2) * width, 128)
                        copies.append(
                            pltpu.make_async_copy(
                                pieces[p].at[s, m, :, pl.ds(start + i * width, width)],
                                ref.at[pl.ds(row, 64), pl.ds(col, width)],
                                sems.at[len(copies)],
                            )
                        )
    return copies


def rms(values):
    return lax.rsqrt(jnp.mean(values * values, axis=-1, keepdims=True) + EPS)


def call(kernel, outs, in_specs, scratch, args, flops=0, traffic=0, vmem=24):
    return pl.pallas_call(
        kernel,
        out_shape=tuple(jax.ShapeDtypeStruct(shape, dtype) for shape, dtype in outs),
        in_specs=in_specs,
        out_specs=(SPACE_VMEM,) * len(outs),
        scratch_shapes=scratch,
        cost_estimate=pl.CostEstimate(flops=flops, bytes_accessed=traffic, transcendentals=0),
        compiler_params=pltpu.CompilerParams(vmem_limit_bytes=vmem * 2**20),
    )(*args)


def mixer_forward_kernel(*refs):
    blocks, behind, gain, taps, length = refs[:4], refs[4], refs[5], refs[6], refs[7]
    pieces = refs[8:10]
    parts = refs[10:14]
    normed, proj, conv, prod, scale, gated, win, wout = refs[14:22]
    wide, sems = refs[22:]
    _, _, _, z = position()
    copies = grouped_copies(pieces, ((win, 0, 3, 128), (wout, 384, 1, 128)), sems)
    for c in copies:
        c.start()

    def scaled(values):
        return (values * rms(values) * gain[...]).astype(BF16)

    for m in range(4):
        values = blocks[m][:128, :].astype(F32)
        inverse = rms(values)
        rows = (values * inverse * gain[...]).astype(BF16)
        wide[m * 144 + 16 : (m + 1) * 144, :] = rows
        normed[m * 128 : (m + 1) * 128, :] = rows
        scale[m * 128 : (m + 1) * 128, :] = inverse
    outside = scaled(behind[...].astype(F32))
    for m in range(4):
        here = z ^ m
        at = pl.multiple_of(((here + 3) % 4 ^ z) * 128 + 112, 16)
        wide[m * 144 : m * 144 + 16, :] = jnp.where(here > 0, normed[pl.ds(at, 16), :], outside)
    for c in copies:
        c.wait()
    out = jnp.dot(wide[...], win[...], preferred_element_type=F32)
    for m in range(4):
        rows = slice(m * 128, (m + 1) * 128)
        here = out[m * 144 : (m + 1) * 144]
        proj[rows, :] = here[16:]
        product = (here[:, :256] * here[:, 512:]).astype(BF16).astype(F32)
        prod[m] = product
        places = first_token(m) + lax.broadcasted_iota(jnp.int32, (128, 256), 0)
        live = places < length[0, 0]
        one = jnp.where((places >= 1) & live, 1.0, 0.0)
        two = jnp.where((places >= 2) & live, 1.0, 0.0)
        conv_out = (
            taps[2:3, :] * product[16:]
            + one * (taps[1:2, :] * product[15:143])
            + two * (taps[0:1, :] * product[14:142])
        )
        conv[rows, :] = conv_out
        gated[rows, :] = (here[16:, 256:512] * conv_out).astype(BF16)
    out = lax.dot_general(gated[...], wout[...], CONTRACT_LAST, preferred_element_type=F32)
    for m in range(4):
        parts[m][...] = out[m * 128 : (m + 1) * 128].astype(BF16)


def mixer_forward(blocks, behind, gain, taps, length, pieces):
    out = call(
        mixer_forward_kernel,
        (
            *[((128, 1024), BF16)] * 4,
            ((512, 1024), BF16),
            ((512, 768), F32),
            ((512, 256), F32),
            ((4, 144, 256), F32),
            ((512, 1), F32),
            ((512, 256), BF16),
            ((1024, 768), BF16),
            ((1024, 256), BF16),
        ),
        [SPACE_VMEM] * 7 + [SPACE_SMEM] + [SPACE_ANY] * 2,
        [pltpu.VMEM((576, 1024), BF16), pltpu.SemaphoreType.DMA((128,))],
        (*blocks, behind, gain, taps, length, *pieces),
        flops=2 * 576 * 1024 * 1024,
        traffic=2**23,
    )
    return out[:4], *out[4:]


def ffn_kernel(*refs):
    n_blocks, c_blocks, pieces = refs[:4], refs[4:8], refs[8:14]
    d_two, d_gu, act = refs[14:18], refs[18], refs[19]
    weights, normed, cot, sems = refs[20:]
    copies = weight_copies(pieces, ((weights, 0, 3, FF_PAD),), sems)
    for c in copies:
        c.start()
    for m in range(4):
        normed[m * 128 : (m + 1) * 128, :] = n_blocks[m][...]
        cot[m * 128 : (m + 1) * 128, :] = c_blocks[m][128:, :]
    wide = 2 * FF_PAD
    results = []
    for i, left in enumerate((normed, normed, cot)):
        for c in copies[i * 32 : (i + 1) * 32]:
            c.wait()
        cols = slice(i * wide, (i + 1) * wide)
        results.append(jnp.dot(left[...], weights[:, cols], preferred_element_type=F32))
    gate, up, da = results
    sig = jax.nn.sigmoid(gate)
    swish = gate * sig
    d_gate = (da * up * sig * (1.0 + gate * (1.0 - sig))).astype(BF16)
    d_up = (da * swish).astype(BF16)
    act[...] = (swish * up).astype(BF16)
    d_gu[:, :wide] = d_gate
    d_gu[:, wide:] = d_up
    total = lax.dot_general(
        d_gu[...], weights[:, : 2 * wide], CONTRACT_LAST, preferred_element_type=F32
    )
    for m in range(4):
        d_two[m][...] = total[m * 128 : (m + 1) * 128, :].astype(BF16)


def ffn_block(n_blocks, c_blocks, pieces):
    out = call(
        ffn_kernel,
        (
            *[((128, 1024), BF16)] * 4,
            ((512, 4 * FF_PAD), BF16),
            ((512, 2 * FF_PAD), BF16),
        ),
        [SPACE_VMEM] * 8 + [SPACE_ANY] * 6,
        [
            pltpu.VMEM((1024, 6 * FF_PAD), BF16),
            pltpu.VMEM((512, 1024), BF16),
            pltpu.VMEM((512, 1024), BF16),
            pltpu.SemaphoreType.DMA((96,)),
        ],
        (*n_blocks, *c_blocks, *pieces),
        flops=2 * 512 * 1024 * 6 * FF_PAD * 2,
        traffic=2**24,
        vmem=40,
    )
    return out[:4], *out[4:]


def down_kernel(*refs):
    act, pieces, outs = refs[0], refs[1:7], refs[7:11]
    weights, sems = refs[11:]
    copies = weight_copies(pieces, ((weights, 2 * FF_PAD, 1, FF_PAD),), sems)
    for c in copies:
        c.start()
    for c in copies:
        c.wait()
    product = lax.dot_general(act[...], weights[...], CONTRACT_LAST, preferred_element_type=F32)
    for m in range(4):
        outs[m][...] = product[m * 128 : (m + 1) * 128].astype(BF16)


def down_projection(act, pieces):
    return call(
        down_kernel,
        (((128, 1024), BF16),) * 4,
        [SPACE_VMEM] + [SPACE_ANY] * 6,
        [pltpu.VMEM((1024, 2 * FF_PAD), BF16), pltpu.SemaphoreType.DMA((32,))],
        (act, *pieces),
        flops=2 * 512 * 1024 * 2 * FF_PAD,
        traffic=2**22,
    )


def grads_kernel(mode, width, pairs, *refs):
    received = None if mode == "other" else refs[0]
    outs, turned, full = refs[-6:-2], refs[-2], refs[-1]
    x, core, y, _ = position()
    carrier = 1 - core if mode == "other" else core
    owners = (core, 1 - core) if mode == "both" else (carrier,)
    at = 0
    for lefts, right in pairs:
        for b, owner in enumerate(owners):
            for x_to in range(4):
                lanes = pl.ds(pl.multiple_of((x_to * 2 + owner) * 128, 128), 128)
                first = b * 512 + x_to * 128
                token = 0
                for left, skip in lefts:
                    count = left.shape[0] - skip
                    turned[first : first + 128, token : token + count] = left[skip:, lanes].T
                    token += count
        for i in range(right.shape[1] // (2 * width)):
            full[:, at : at + 2 * width] = jnp.dot(
                turned[...],
                right[:, i * 2 * width : (i + 1) * 2 * width],
                preferred_element_type=F32,
            ).astype(BF16)
            at += 2 * width
    count = at // (2 * width)
    for s in range(4):
        for f in range(4):
            x_to = x ^ jnp.where(carrier == 0, f, s)
            y_to = y ^ jnp.where(carrier == 0, s, f)
            for b in range(len(owners)):
                rows = pl.ds(pl.multiple_of(b * 512 + x_to * 128 + (y_to % 2) * 64, 64), 64)
                for i in range(count):
                    cols = pl.ds(pl.multiple_of((i * 2 + y_to // 2) * width, 128), width)
                    here = slice((b * count + i) * width, (b * count + i + 1) * width)
                    piece = full[rows, cols]
                    if mode == "own":
                        piece = (piece.astype(F32) + received[s, f, :, here].astype(F32)).astype(BF16)
                    if mode == "other":
                        outs[0][s, f, :, here] = piece
                    elif mode == "own":
                        outs[s][f, :, here] = piece
                    else:
                        outs[s][f * 64 : (f + 1) * 64, here] = piece
        if mode == "both":
            outs[s][256:, :] = received[...]


def grads_half(pairs, width, mode, received=None):
    total = sum(right.shape[1] for _, right in pairs) // 2
    cores = 2 if mode == "both" else 1
    args = [v for lefts, right in pairs for v in (*(left for left, _ in lefts), right)]

    def kernel(*refs):
        given, at = [], 0
        for lefts, _ in pairs:
            count = len(lefts)
            skips = [skip for _, skip in lefts]
            given.append((list(zip(refs[at : at + count], skips)), refs[at + count]))
            at += count + 1
        rest = refs[at:]
        if mode == "other":
            rest = (rest[0], None, None, None, *rest[1:])
        grads_kernel(mode, width, given, *rest)

    out = call(
        kernel,
        {
            "other": (((4, 4, 64, total), BF16),),
            "own": (((4, 64, total), BF16),) * 4,
            "both": (((272, 2 * total), BF16),) * 4,
        }[mode],
        [SPACE_VMEM] * (len(args) + (mode != "other")),
        [pltpu.VMEM((cores * 512, 512), BF16), pltpu.VMEM((cores * 512, 2 * total), BF16)],
        (*args, *(() if mode == "other" else (received,))),
        flops=2 * 512 * 512 * total * 2,
        traffic=2**23,
        vmem=32,
    )
    return out[0] if mode == "other" else out


def second_sum(own, got):
    return sum(v.astype(F32) for v in (own, got[1], got[2], got[3]))


def scatter_first(parts, small=None):
    width = sum(p.shape[2] for p in parts)
    extra = [] if small is None else [split_rows(small, 64, 256)]
    last = {
        m: first_axis(jnp.concatenate([*(p[m].astype(BF16) for p in parts), *extra], axis=1), m)
        for m in (2, 1, 3)
    }
    came = sum(last[m].astype(F32) for m in (1, 2, 3))
    out, at = [], 0
    for p in parts:
        out.append(p[0] + came[:, at : at + p.shape[2]])
        at += p.shape[2]
    if small is None:
        return out
    return out, small + joined_rows(came[:, width:], small.shape)


def mixer_pull_kernel(*refs):
    blocks, proj, conv, wout = refs[:4], refs[4], refs[5], refs[6]
    d_conv, d_c, d_mixer = refs[7:]
    for m in range(4):
        d_mixer[m * 128 : (m + 1) * 128, :] = blocks[m][...]
    d_gated = jnp.dot(d_mixer[...], wout[...], preferred_element_type=F32)
    d_conv[...] = (d_gated * proj[:, 256:512]).astype(BF16)
    d_c[...] = (d_gated * conv[...]).astype(BF16)


def mixer_pull(blocks, proj, conv, wout):
    return call(
        mixer_pull_kernel,
        (((512, 256), BF16), ((512, 256), BF16)),
        [SPACE_VMEM] * 7,
        [pltpu.VMEM((512, 1024), BF16)],
        (*blocks, proj, conv, wout),
        flops=2 * 512 * 1024 * 256,
        traffic=2**21,
    )


def mixer_backward_kernel(*refs):
    blocks = refs[:4]
    d_conv, d_c, outside, proj, prod, scale, taps, length, win, gain_two = refs[4:14]
    sent = refs[14:18]
    d_proj, extra, small = refs[18:]
    _, _, _, z = position()
    small[...] = jnp.zeros((5, 1024), F32)
    sums = [0.0, 0.0, 0.0]
    for m in range(4):
        here = z ^ m
        rows = slice(m * 128, (m + 1) * 128)
        at = pl.multiple_of(((here + 1) % 4 ^ z) * 128, 128)
        inner = d_conv[pl.ds(at, 16), :].astype(F32)
        following = jnp.where(here < 3, inner, outside[...].astype(F32))
        places = first_token(m) + lax.broadcasted_iota(jnp.int32, (128, 256), 0)
        live = places < length[0, 0]
        one = jnp.where((places >= 1) & live, 1.0, 0.0)
        two = jnp.where((places >= 2) & live, 1.0, 0.0)
        one_back = jnp.where(places + 1 < length[0, 0], 1.0, 0.0)
        two_back = jnp.where(places + 2 < length[0, 0], 1.0, 0.0)
        pull = d_conv[rows, :].astype(F32)
        longer = jnp.concatenate([pull, following], axis=0)
        d_product = (
            taps[2:3, :] * pull
            + one_back * (taps[1:2, :] * longer[1:129])
            + two_back * (taps[0:1, :] * longer[2:130])
        )
        d_proj[rows, :256] = (d_product * proj[rows, 512:]).astype(BF16)
        d_proj[rows, 256:512] = d_c[rows, :]
        d_proj[rows, 512:] = (d_product * proj[rows, :256]).astype(BF16)
        sums[0] += jnp.sum(pull * two * prod[m, 14:142, :], axis=0, keepdims=True)
        sums[1] += jnp.sum(pull * one * prod[m, 15:143, :], axis=0, keepdims=True)
        sums[2] += jnp.sum(pull * prod[m, 16:, :], axis=0, keepdims=True)
    for h in range(2):
        lanes = pl.ds(pl.multiple_of((h * 4 + z) * 128, 128), 128)
        for i in range(3):
            small[2 + i : 3 + i, lanes] = sums[i][:, h * 128 : (h + 1) * 128]
    out = lax.dot_general(d_proj[...], win[...], CONTRACT_LAST, preferred_element_type=F32)
    gain = 0.0
    for m in range(4):
        rows = slice(m * 128, (m + 1) * 128)
        unit = blocks[m][:128, :].astype(F32) * scale[rows, :]
        gain += jnp.sum(out[rows] * unit, axis=0, keepdims=True)
        sent[m][...] = out[rows].astype(BF16)
    small[0:1, :] = gain
    small[1:2, :] = gain_two[...]
    high = small[...].astype(BF16)
    low = (small[...] - high.astype(F32)).astype(BF16)
    rows = jnp.concatenate([high.astype(F32), low.astype(F32), jnp.zeros((6, 1024), F32)], axis=0)
    extra[...] = rows.astype(BF16)


def mixer_backward(
    blocks, d_conv, d_c, outside, proj, prod, scale, taps, length, win, gain_two
):
    out = call(
        mixer_backward_kernel,
        (
            *[((128, 1024), BF16)] * 4,
            ((512, 768), BF16),
            ((16, 1024), BF16),
        ),
        [SPACE_VMEM] * 11 + [SPACE_SMEM] + [SPACE_VMEM] * 2,
        [pltpu.VMEM((5, 1024), F32)],
        (*blocks, d_conv, d_c, outside, proj, prod, scale, taps, length, win, gain_two),
        flops=2 * 512 * 1024 * 768,
        traffic=2**23,
    )
    return out[:4], out[4], out[5]


def body(tokens, lengths, gain_one, w_in, conv_weight, w_out, gain_two, w_gu, w_down, cotangent):
    z = lax.axis_index("z")
    tail = jnp.zeros((64, FF_PAD - FF_BLOCK), BF16)
    pack = jnp.concatenate(
        [w_in[:, 0], w_in[:, 1], w_in[:, 2], w_out.T]
        + [w_gu[0], tail, w_gu[1], tail, w_down.T, tail],
        axis=1,
    )
    first = all_first(pack)
    blocks = all_z(jnp.concatenate([tokens, cotangent], axis=0))
    mixer_mine = grouped_second(jnp.stack([v[:, :512] for v in first]))
    ends = jnp.stack([v[112:128] for v in blocks])
    behind = from_group(lax.dynamic_index_in_dim(ends, 3 ^ z, 0, keepdims=False), -1)
    behind, mixer_mine, ffn_first = together(
        behind, mixer_mine, jnp.stack([v[:, 512:] for v in first])
    )
    mixer_pieces = (mixer_mine, other_core(mixer_mine))
    ffn_got = {m: second_axis(ffn_first, m) for m in (1, 3)}
    taps = jnp.concatenate(
        [
            lax.dynamic_slice_in_dim(conv_weight, z * 128, 128, 1),
            lax.dynamic_slice_in_dim(conv_weight, 512 + z * 128, 128, 1),
        ],
        axis=1,
    )
    residual = tokens.astype(F32)

    part, normed_one, proj, conv, prod, scale_one, gated, win, wout = mixer_forward(
        blocks, behind, gain_one[None], taps, lengths, mixer_pieces
    )
    part, ffn_got, ffn_first = together(part, ffn_got, ffn_first)
    ffn_got[2] = second_axis(ffn_first, 2)
    middle = residual + sum_z(part)
    ffn_got, middle = together(ffn_got, middle)
    ffn_mine = [ffn_first, ffn_got[1], ffn_got[2], ffn_got[3]]
    scale_two = rms(middle)
    unit_two = middle * scale_two
    normed_own = (unit_two * gain_two).astype(BF16)
    ffn_pieces = both_cores(ffn_mine)
    normed_two = all_z(normed_own)

    d_two, d_gu, activation = ffn_block(
        normed_two, blocks, ffn_pieces
    )
    ffn_pairs = [
        ([(v, 0) for v in normed_two], d_gu),
        ([(v, 128) for v in blocks], activation),
    ]
    ffn_sent = grads_half(ffn_pairs, FF_PAD, "other")
    d_normed_two = sum_z(d_two)
    pulled = d_normed_two * gain_two
    d_middle = cotangent.astype(F32) + scale_two * (
        pulled - unit_two * jnp.mean(pulled * unit_two, axis=-1, keepdims=True)
    )
    gain_two_part = jnp.sum(d_normed_two * unit_two, axis=0)
    ffn_sent, d_mixer_own = together(ffn_sent, d_middle.astype(BF16))
    d_mixer_blocks = all_z(d_mixer_own)
    ffn_half = grads_half(ffn_pairs, FF_PAD, "own", other_core(ffn_sent))
    ffn_half, d_mixer_blocks = together(ffn_half, d_mixer_blocks)

    d_conv, d_c = mixer_pull(d_mixer_blocks, proj, conv, wout)
    d_conv, act_late = together(d_conv, activation)
    outside = from_group(lax.dynamic_slice_in_dim(d_conv, z * 128, 16, 0), 1)
    ffn = down_projection(act_late, ffn_pieces)
    outside, ffn, ffn_half = together(outside, ffn, ffn_half)
    ffn_got = {m: second_axis(ffn_half[m], m) for m in (1, 3)}
    sent, d_projected, extra = mixer_backward(
        blocks, d_conv, d_c, outside, proj, prod, scale_one, taps, lengths, win,
        gain_two_part[None],
    )
    mixer_pairs = [
        ([(normed_one, 0)], d_projected),
        ([(v, 0) for v in d_mixer_blocks], gated),
    ]
    mixer_half = grads_half(mixer_pairs, 128, "both", extra)
    mixer_half, ffn_got, ffn_half = together(mixer_half, ffn_got, ffn_half)
    ffn_got[2] = second_axis(ffn_half[2], 2)
    mixer_got = {m: second_axis(mixer_half[m], m) for m in (2, 1, 3)}
    d_normed_one = sum_z(sent)
    mixer_got, ffn_got, ffn, d_normed_one = together(mixer_got, ffn_got, ffn, d_normed_one)
    ffn_out = sum_z(ffn)
    mixed = (middle + ffn_out).astype(BF16)
    ffn_total = second_sum(ffn_half[0], ffn_got)
    mixer_total = second_sum(mixer_half[0], mixer_got)
    small = mixer_total[256:261] + mixer_total[261:266]
    (mixer_both, ffn_grads), small = scatter_first(
        [mixer_total[:256].reshape(4, 64, 1024), ffn_total], small
    )
    small = small + other_core(small)
    small = small + sum(along_z(small, m) for m in (2, 1, 3))
    mixer_grads = mixer_both[:, :512] + other_core(mixer_both[:, 512:].astype(BF16)).astype(F32)

    scale_own = rms(residual)
    unit_one = residual * scale_own
    pulled_one = d_normed_one * gain_one
    grad_tokens = d_middle + scale_own * (
        pulled_one - unit_one * jnp.mean(pulled_one * unit_one, axis=-1, keepdims=True)
    )

    return (
        mixed,
        grad_tokens,
        small[0],
        mixer_grads[:, :384].reshape(64, 3, 128),
        small[2:],
        mixer_grads[:, 384:].T,
        small[1],
        jnp.stack([ffn_grads[:, :FF_BLOCK], ffn_grads[:, FF_PAD : FF_PAD + FF_BLOCK]]),
        ffn_grads[:, 2 * FF_PAD : 2 * FF_PAD + FF_BLOCK].T,
    )


def solution(mesh):
    fine = Mesh(mesh.devices.reshape(SIZES), AXES)
    rows = P(AXES, None)
    fsdp_ctx = ("x", "core", "ylo")
    tp = ("yhi", "z")
    return jax.shard_map(
        body,
        mesh=fine,
        in_specs=(
            rows,
            P(("x", "core"), None),
            P(),
            P(fsdp_ctx, None, tp),
            P(),
            P(tp, fsdp_ctx),
            P(),
            P(None, fsdp_ctx, tp),
            P(tp, fsdp_ctx),
            rows,
        ),
        out_specs=(
            rows,
            rows,
            P(),
            P(fsdp_ctx, None, tp),
            P(),
            P(tp, fsdp_ctx),
            P(),
            P(None, fsdp_ctx, tp),
            P(tp, fsdp_ctx),
        ),
        check_vma=False,
    )
```

```python
import jax
import jax.numpy as jnp
from jax import lax
from jax.experimental import pallas as pl
from jax.experimental.pallas import tpu as pltpu
from jax.sharding import Mesh
from jax.sharding import PartitionSpec as P

EPS = 1e-05
F32 = jnp.float32
BF16 = jnp.bfloat16
AXES = ("x", "core", "ylo", "yhi", "z")
SIZES = (4, 2, 2, 2, 4)
SPACE_ANY = pl.BlockSpec(memory_space=pl.ANY)
SPACE_VMEM = pl.BlockSpec(memory_space=pltpu.VMEM)
SPACE_SMEM = pl.BlockSpec(memory_space=pltpu.SMEM)
CONTRACT_LAST = (((1,), (1,)), ((), ()))
CONTRACT_FIRST = (((0,), (0,)), ((), ()))
FF_BLOCK = 576
FF_PAD = 640


def device_number(x, core, y, z):
    return (((x * 2 + core) * 2 + y % 2) * 2 + y // 2) * 4 + z


def route(step):
    return [
        (device_number(x, core, y, z), device_number(*step(x, core, y, z)))
        for x in range(4)
        for core in range(2)
        for y in range(4)
        for z in range(4)
    ]


def along_z(value, m):
    return lax.ppermute(value, AXES, route(lambda x, c, y, z: (x, c, y, z ^ m)))


def along_x(value, m):
    return lax.ppermute(value, AXES, route(lambda x, c, y, z: (x ^ m, c, y, z)))


def along_y(value, m):
    return lax.ppermute(value, AXES, route(lambda x, c, y, z: (x, c, y ^ m, z)))


def other_core(value):
    return lax.ppermute(value, AXES, route(lambda x, c, y, z: (x, 1 - c, y, z)))


def first_axis(value, m):
    def step(x, c, y, z):
        return (x ^ m, c, y, z) if c == 0 else (x, c, y ^ m, z)

    return lax.ppermute(value, AXES, route(step))


def second_axis(value, m):
    def step(x, c, y, z):
        return (x, c, y ^ m, z) if c == 0 else (x ^ m, c, y, z)

    return lax.ppermute(value, AXES, route(step))


def second_groups():
    groups = [
        [device_number(x, 0, y, z) for y in range(4)] for x in range(4) for z in range(4)
    ]
    return groups + [
        [device_number(x, 1, y, z) for x in range(4)] for y in range(4) for z in range(4)
    ]


def grouped_second(own):
    spread = jnp.broadcast_to(own[None], (4, *own.shape))
    return lax.all_to_all(spread, AXES, 0, 0, axis_index_groups=second_groups())


def together(*values):
    return lax.optimization_barrier(values)


def all_z(own):
    got = {m: along_z(own, m) for m in (2, 1, 3)}
    return [own, got[1], got[2], got[3]]


def sum_z(blocks):
    got = {m: along_z(blocks[m], m) for m in (2, 1, 3)}
    return sum(v.astype(F32) for v in (blocks[0], got[1], got[2], got[3]))


def all_first(own):
    got = {m: first_axis(own, m) for m in (2, 1, 3)}
    return [own, got[1], got[2], got[3]]


def all_second(own):
    got = {m: second_axis(own, m) for m in (2, 1, 3)}
    return [own, got[1], got[2], got[3]]


def both_cores(pieces):
    return [*pieces, other_core(pieces[0]), other_core(jnp.stack(pieces[1:]))]


def split_rows(vector, rows, width):
    high = lax.reduce_precision(vector, 8, 7)
    both = jnp.stack([high.astype(BF16), (vector - high).astype(BF16)]).reshape(-1, width)
    return jnp.pad(both, ((0, rows - both.shape[0]), (0, 0)))


def joined_rows(rows, shape):
    count = shape[0] * shape[1] // rows.shape[1]
    return (rows[:count] + rows[count : 2 * count]).reshape(shape)


def from_group(block, shift):
    pairs = []
    for x in range(4):
        for c in range(2):
            for y in range(4):
                for z in range(4):
                    to = (y % 2) * 2 + y // 2 - shift
                    if 0 <= to < 4:
                        target = device_number(x, c, (to % 2) * 2 + to // 2, z)
                        pairs.append((device_number(x, c, y, z), target))
    return lax.ppermute(block, AXES, pairs)


def position():
    y = lax.axis_index("yhi") * 2 + lax.axis_index("ylo")
    return lax.axis_index("x"), lax.axis_index("core"), y, lax.axis_index("z")


def first_token(m):
    _, _, y, z = position()
    return (((y % 2) * 2 + y // 2) * 4 + (z ^ m)) * 128


def weight_copies(pieces, targets, sems):
    x, core, y, _ = position()
    sources = [*pieces[:5], *(pieces[5].at[i] for i in range(3))]
    copies = []
    for ref, start, count, width in targets:
        for i in range(count):
            for p in range(8):
                k = core if p < 4 else 1 - core
                for m in range(4):
                    x_from = jnp.where(k == 0, x ^ m, x ^ (p % 4))
                    y_from = jnp.where(k == 0, y ^ (p % 4), y ^ m)
                    row = pl.multiple_of(((x_from * 2 + k) * 2 + y_from % 2) * 64, 64)
                    col = pl.multiple_of((i * 2 + y_from // 2) * width, 128)
                    copies.append(
                        pltpu.make_async_copy(
                            sources[p].at[m, :, pl.ds(start + i * width, width)],
                            ref.at[pl.ds(row, 64), pl.ds(col, width)],
                            sems.at[len(copies)],
                        )
                    )
    return copies


def grouped_copies(pieces, targets, sems):
    x, core, y, _ = position()
    copies = []
    for p in range(2):
        k = core if p == 0 else 1 - core
        for s in range(4):
            for m in range(4):
                x_from = jnp.where(k == 0, x ^ m, s)
                y_from = jnp.where(k == 0, s, y ^ m)
                row = pl.multiple_of(((x_from * 2 + k) * 2 + y_from % 2) * 64, 64)
                for ref, start, count, width in targets:
                    for i in range(count):
                        col = pl.multiple_of((i * 2 + y_from // 2) * width, 128)
                        copies.append(
                            pltpu.make_async_copy(
                                pieces[p].at[s, m, :, pl.ds(start + i * width, width)],
                                ref.at[pl.ds(row, 64), pl.ds(col, width)],
                                sems.at[len(copies)],
                            )
                        )
    return copies


def rms(values):
    return lax.rsqrt(jnp.mean(values * values, axis=-1, keepdims=True) + EPS)


def call(kernel, outs, in_specs, scratch, args, flops=0, traffic=0, vmem=14):
    return pl.pallas_call(
        kernel,
        out_shape=tuple(jax.ShapeDtypeStruct(shape, dtype) for shape, dtype in outs),
        in_specs=in_specs,
        out_specs=(SPACE_VMEM,) * len(outs),
        scratch_shapes=scratch,
        cost_estimate=pl.CostEstimate(flops=flops, bytes_accessed=traffic, transcendentals=0),
        compiler_params=pltpu.CompilerParams(vmem_limit_bytes=vmem * 2**20),
    )(*args)


def mixer_forward_kernel(*refs):
    blocks, behind, gain, taps, length = refs[:4], refs[4], refs[5], refs[6], refs[7]
    pieces = refs[8:10]
    parts = refs[10:14]
    normed, proj, conv, prod, scale, gated, win, wout = refs[14:22]
    wide, sems = refs[22:]
    _, _, _, z = position()
    copies = grouped_copies(pieces, ((win, 0, 3, 128), (wout, 384, 1, 128)), sems)
    for c in copies:
        c.start()

    def scaled(values):
        return (values * rms(values) * gain[...]).astype(BF16)

    for m in range(4):
        values = blocks[m][:128, :].astype(F32)
        inverse = rms(values)
        rows = (values * inverse * gain[...]).astype(BF16)
        wide[m * 144 + 16 : (m + 1) * 144, :] = rows
        normed[m * 128 : (m + 1) * 128, :] = rows
        scale[m * 128 : (m + 1) * 128, :] = inverse
    outside = scaled(behind[...].astype(F32))
    for m in range(4):
        here = z ^ m
        at = pl.multiple_of(((here + 3) % 4 ^ z) * 128 + 112, 16)
        wide[m * 144 : m * 144 + 16, :] = jnp.where(here > 0, normed[pl.ds(at, 16), :], outside)
    for c in copies:
        c.wait()
    out = jnp.dot(wide[...], win[...], preferred_element_type=F32)
    for m in range(4):
        rows = slice(m * 128, (m + 1) * 128)
        here = out[m * 144 : (m + 1) * 144]
        proj[rows, :] = here[16:]
        product = (here[:, :256] * here[:, 512:]).astype(BF16).astype(F32)
        prod[m] = product
        places = first_token(m) + lax.broadcasted_iota(jnp.int32, (128, 256), 0)
        live = places < length[0, 0]
        one = jnp.where((places >= 1) & live, 1.0, 0.0)
        two = jnp.where((places >= 2) & live, 1.0, 0.0)
        conv_out = (
            taps[2:3, :] * product[16:]
            + one * (taps[1:2, :] * product[15:143])
            + two * (taps[0:1, :] * product[14:142])
        )
        conv[rows, :] = conv_out
        gated[rows, :] = (here[16:, 256:512] * conv_out).astype(BF16)
    out = lax.dot_general(gated[...], wout[...], CONTRACT_LAST, preferred_element_type=F32)
    for m in range(4):
        parts[m][...] = out[m * 128 : (m + 1) * 128].astype(BF16)


def mixer_forward(blocks, behind, gain, taps, length, pieces):
    out = call(
        mixer_forward_kernel,
        (
            *[((128, 1024), BF16)] * 4,
            ((512, 1024), BF16),
            ((512, 768), F32),
            ((512, 256), F32),
            ((4, 144, 256), F32),
            ((512, 1), F32),
            ((512, 256), BF16),
            ((1024, 768), BF16),
            ((1024, 256), BF16),
        ),
        [SPACE_VMEM] * 7 + [SPACE_SMEM] + [SPACE_ANY] * 2,
        [pltpu.VMEM((576, 1024), BF16), pltpu.SemaphoreType.DMA((128,))],
        (*blocks, behind, gain, taps, length, *pieces),
        flops=2 * 576 * 1024 * 1024,
        traffic=2**23,
    )
    return out[:4], *out[4:]


def ffn_kernel(*refs):
    n_blocks, c_blocks, pieces = refs[:4], refs[4:8], refs[8:14]
    d_two, d_gu, act = refs[14:18], refs[18], refs[19]
    weights, normed, cot, sems = refs[20:]
    copies = weight_copies(pieces, ((weights, 0, 3, FF_PAD),), sems)
    for c in copies:
        c.start()
    for m in range(4):
        normed[m * 128 : (m + 1) * 128, :] = n_blocks[m][...]
        cot[m * 128 : (m + 1) * 128, :] = c_blocks[m][128:, :]
    wide = 2 * FF_PAD
    results = []
    for i, left in enumerate((normed, normed, cot)):
        for c in copies[i * 32 : (i + 1) * 32]:
            c.wait()
        cols = slice(i * wide, (i + 1) * wide)
        results.append(jnp.dot(left[...], weights[:, cols], preferred_element_type=F32))
    gate, up, da = results
    sig = jax.nn.sigmoid(gate)
    swish = gate * sig
    d_gate = (da * up * sig * (1.0 + gate * (1.0 - sig))).astype(BF16)
    d_up = (da * swish).astype(BF16)
    act[...] = (swish * up).astype(BF16)
    d_gu[:, :wide] = d_gate
    d_gu[:, wide:] = d_up
    total = lax.dot_general(
        d_gu[...], weights[:, : 2 * wide], CONTRACT_LAST, preferred_element_type=F32
    )
    for m in range(4):
        d_two[m][...] = total[m * 128 : (m + 1) * 128, :].astype(BF16)


def ffn_block(n_blocks, c_blocks, pieces):
    out = call(
        ffn_kernel,
        (
            *[((128, 1024), BF16)] * 4,
            ((512, 4 * FF_PAD), BF16),
            ((512, 2 * FF_PAD), BF16),
        ),
        [SPACE_VMEM] * 8 + [SPACE_ANY] * 6,
        [
            pltpu.VMEM((1024, 6 * FF_PAD), BF16),
            pltpu.VMEM((512, 1024), BF16),
            pltpu.VMEM((512, 1024), BF16),
            pltpu.SemaphoreType.DMA((96,)),
        ],
        (*n_blocks, *c_blocks, *pieces),
        flops=2 * 512 * 1024 * 6 * FF_PAD * 2,
        traffic=2**24,
        vmem=32,
    )
    return out[:4], *out[4:]


def down_kernel(*refs):
    act, pieces, outs = refs[0], refs[1:7], refs[7:11]
    weights, sems = refs[11:]
    copies = weight_copies(pieces, ((weights, 2 * FF_PAD, 1, FF_PAD),), sems)
    for c in copies:
        c.start()
    for c in copies:
        c.wait()
    product = lax.dot_general(act[...], weights[...], CONTRACT_LAST, preferred_element_type=F32)
    for m in range(4):
        outs[m][...] = product[m * 128 : (m + 1) * 128].astype(BF16)


def down_projection(act, pieces):
    return call(
        down_kernel,
        (((128, 1024), BF16),) * 4,
        [SPACE_VMEM] + [SPACE_ANY] * 6,
        [pltpu.VMEM((1024, 2 * FF_PAD), BF16), pltpu.SemaphoreType.DMA((32,))],
        (act, *pieces),
        flops=2 * 512 * 1024 * 2 * FF_PAD,
        traffic=2**22,
    )


def grads_kernel(mode, width, pairs, *refs):
    received = None if mode == "other" else refs[0]
    outs, turned, full = refs[-6:-2], refs[-2], refs[-1]
    x, core, y, _ = position()
    carrier = 1 - core if mode == "other" else core
    owners = (core, 1 - core) if mode == "both" else (carrier,)
    at = 0
    for lefts, right in pairs:
        for b, owner in enumerate(owners):
            for x_to in range(4):
                lanes = pl.ds(pl.multiple_of((x_to * 2 + owner) * 128, 128), 128)
                first = b * 512 + x_to * 128
                token = 0
                for left, skip in lefts:
                    count = left.shape[0] - skip
                    turned[first : first + 128, token : token + count] = left[skip:, lanes].T
                    token += count
        for i in range(right.shape[1] // (2 * width)):
            full[:, at : at + 2 * width] = jnp.dot(
                turned[...],
                right[:, i * 2 * width : (i + 1) * 2 * width],
                preferred_element_type=F32,
            ).astype(BF16)
            at += 2 * width
    count = at // (2 * width)
    for s in range(4):
        for f in range(4):
            x_to = x ^ jnp.where(carrier == 0, f, s)
            y_to = y ^ jnp.where(carrier == 0, s, f)
            for b in range(len(owners)):
                rows = pl.ds(pl.multiple_of(b * 512 + x_to * 128 + (y_to % 2) * 64, 64), 64)
                for i in range(count):
                    cols = pl.ds(pl.multiple_of((i * 2 + y_to // 2) * width, 128), width)
                    here = slice((b * count + i) * width, (b * count + i + 1) * width)
                    piece = full[rows, cols]
                    if mode == "own":
                        piece = (piece.astype(F32) + received[s, f, :, here].astype(F32)).astype(BF16)
                    if mode == "other":
                        outs[0][s, f, :, here] = piece
                    elif mode == "own":
                        outs[s][f, :, here] = piece
                    else:
                        outs[s][f * 64 : (f + 1) * 64, here] = piece
        if mode == "both":
            outs[s][256:, :] = received[...]


def grads_half(pairs, width, mode, received=None):
    total = sum(right.shape[1] for _, right in pairs) // 2
    cores = 2 if mode == "both" else 1
    args = [v for lefts, right in pairs for v in (*(left for left, _ in lefts), right)]

    def kernel(*refs):
        given, at = [], 0
        for lefts, _ in pairs:
            count = len(lefts)
            skips = [skip for _, skip in lefts]
            given.append((list(zip(refs[at : at + count], skips)), refs[at + count]))
            at += count + 1
        rest = refs[at:]
        if mode == "other":
            rest = (rest[0], None, None, None, *rest[1:])
        grads_kernel(mode, width, given, *rest)

    out = call(
        kernel,
        {
            "other": (((4, 4, 64, total), BF16),),
            "own": (((4, 64, total), BF16),) * 4,
            "both": (((272, 2 * total), BF16),) * 4,
        }[mode],
        [SPACE_VMEM] * (len(args) + (mode != "other")),
        [pltpu.VMEM((cores * 512, 512), BF16), pltpu.VMEM((cores * 512, 2 * total), BF16)],
        (*args, *(() if mode == "other" else (received,))),
        flops=2 * 512 * 512 * total * 2,
        traffic=2**23,
        vmem=16,
    )
    return out[0] if mode == "other" else out


def second_sum(own, got):
    return sum(v.astype(F32) for v in (own, got[1], got[2], got[3]))


def scatter_first(parts, small=None):
    width = sum(p.shape[2] for p in parts)
    extra = [] if small is None else [split_rows(small, 64, 256)]
    last = {
        m: first_axis(jnp.concatenate([*(p[m].astype(BF16) for p in parts), *extra], axis=1), m)
        for m in (2, 1, 3)
    }
    came = sum(last[m].astype(F32) for m in (1, 2, 3))
    out, at = [], 0
    for p in parts:
        out.append(p[0] + came[:, at : at + p.shape[2]])
        at += p.shape[2]
    if small is None:
        return out
    return out, small + joined_rows(came[:, width:], small.shape)


def mixer_pull_kernel(*refs):
    blocks, proj, conv, wout = refs[:4], refs[4], refs[5], refs[6]
    d_conv, d_c, d_mixer = refs[7:]
    for m in range(4):
        d_mixer[m * 128 : (m + 1) * 128, :] = blocks[m][...]
    d_gated = jnp.dot(d_mixer[...], wout[...], preferred_element_type=F32)
    d_conv[...] = (d_gated * proj[:, 256:512]).astype(BF16)
    d_c[...] = (d_gated * conv[...]).astype(BF16)


def mixer_pull(blocks, proj, conv, wout):
    return call(
        mixer_pull_kernel,
        (((512, 256), BF16), ((512, 256), BF16)),
        [SPACE_VMEM] * 7,
        [pltpu.VMEM((512, 1024), BF16)],
        (*blocks, proj, conv, wout),
        flops=2 * 512 * 1024 * 256,
        traffic=2**21,
        vmem=8,
    )


def mixer_backward_kernel(*refs):
    blocks = refs[:4]
    d_conv, d_c, outside, proj, prod, scale, taps, length, win, gain_two = refs[4:14]
    sent = refs[14:18]
    d_proj, extra, small = refs[18:]
    _, _, _, z = position()
    small[...] = jnp.zeros((5, 1024), F32)
    sums = [0.0, 0.0, 0.0]
    for m in range(4):
        here = z ^ m
        rows = slice(m * 128, (m + 1) * 128)
        at = pl.multiple_of(((here + 1) % 4 ^ z) * 128, 128)
        inner = d_conv[pl.ds(at, 16), :].astype(F32)
        following = jnp.where(here < 3, inner, outside[...].astype(F32))
        places = first_token(m) + lax.broadcasted_iota(jnp.int32, (128, 256), 0)
        live = places < length[0, 0]
        one = jnp.where((places >= 1) & live, 1.0, 0.0)
        two = jnp.where((places >= 2) & live, 1.0, 0.0)
        one_back = jnp.where(places + 1 < length[0, 0], 1.0, 0.0)
        two_back = jnp.where(places + 2 < length[0, 0], 1.0, 0.0)
        pull = d_conv[rows, :].astype(F32)
        longer = jnp.concatenate([pull, following], axis=0)
        d_product = (
            taps[2:3, :] * pull
            + one_back * (taps[1:2, :] * longer[1:129])
            + two_back * (taps[0:1, :] * longer[2:130])
        )
        d_proj[rows, :256] = (d_product * proj[rows, 512:]).astype(BF16)
        d_proj[rows, 256:512] = d_c[rows, :]
        d_proj[rows, 512:] = (d_product * proj[rows, :256]).astype(BF16)
        sums[0] += jnp.sum(pull * two * prod[m, 14:142, :], axis=0, keepdims=True)
        sums[1] += jnp.sum(pull * one * prod[m, 15:143, :], axis=0, keepdims=True)
        sums[2] += jnp.sum(pull * prod[m, 16:, :], axis=0, keepdims=True)
    for h in range(2):
        lanes = pl.ds(pl.multiple_of((h * 4 + z) * 128, 128), 128)
        for i in range(3):
            small[2 + i : 3 + i, lanes] = sums[i][:, h * 128 : (h + 1) * 128]
    out = lax.dot_general(d_proj[...], win[...], CONTRACT_LAST, preferred_element_type=F32)
    gain = 0.0
    for m in range(4):
        rows = slice(m * 128, (m + 1) * 128)
        unit = blocks[m][:128, :].astype(F32) * scale[rows, :]
        gain += jnp.sum(out[rows] * unit, axis=0, keepdims=True)
        sent[m][...] = out[rows].astype(BF16)
    small[0:1, :] = gain
    small[1:2, :] = gain_two[...]
    high = small[...].astype(BF16)
    low = (small[...] - high.astype(F32)).astype(BF16)
    rows = jnp.concatenate([high.astype(F32), low.astype(F32), jnp.zeros((6, 1024), F32)], axis=0)
    extra[...] = rows.astype(BF16)


def mixer_backward(
    blocks, d_conv, d_c, outside, proj, prod, scale, taps, length, win, gain_two
):
    out = call(
        mixer_backward_kernel,
        (
            *[((128, 1024), BF16)] * 4,
            ((512, 768), BF16),
            ((16, 1024), BF16),
        ),
        [SPACE_VMEM] * 11 + [SPACE_SMEM] + [SPACE_VMEM] * 2,
        [pltpu.VMEM((5, 1024), F32)],
        (*blocks, d_conv, d_c, outside, proj, prod, scale, taps, length, win, gain_two),
        flops=2 * 512 * 1024 * 768,
        traffic=2**23,
    )
    return out[:4], out[4], out[5]


def body(tokens, lengths, gain_one, w_in, conv_weight, w_out, gain_two, w_gu, w_down, cotangent):
    z = lax.axis_index("z")
    tail = jnp.zeros((64, FF_PAD - FF_BLOCK), BF16)
    pack = jnp.concatenate(
        [w_in[:, 0], w_in[:, 1], w_in[:, 2], w_out.T]
        + [w_gu[0], tail, w_gu[1], tail, w_down.T, tail],
        axis=1,
    )
    first = all_first(pack)
    blocks = all_z(jnp.concatenate([tokens, cotangent], axis=0))
    mixer_mine = grouped_second(jnp.stack([v[:, :512] for v in first]))
    ends = jnp.stack([v[112:128] for v in blocks])
    behind = from_group(lax.dynamic_index_in_dim(ends, 3 ^ z, 0, keepdims=False), -1)
    mixer_mine, ffn_first = together(mixer_mine, jnp.stack([v[:, 512:] for v in first]))
    mixer_pieces = (mixer_mine, other_core(mixer_mine))
    ffn_got = {m: second_axis(ffn_first, m) for m in (1, 3)}
    behind, ffn_late = together(behind, ffn_first)
    ffn_got[2] = second_axis(ffn_late, 2)
    taps = jnp.concatenate(
        [
            lax.dynamic_slice_in_dim(conv_weight, z * 128, 128, 1),
            lax.dynamic_slice_in_dim(conv_weight, 512 + z * 128, 128, 1),
        ],
        axis=1,
    )
    residual = tokens.astype(F32)

    part, normed_one, proj, conv, prod, scale_one, gated, win, wout = mixer_forward(
        blocks, behind, gain_one[None], taps, lengths, mixer_pieces
    )
    middle = residual + sum_z(part)
    ffn_got, middle = together(ffn_got, middle)
    ffn_mine = [ffn_first, ffn_got[1], ffn_got[2], ffn_got[3]]
    scale_two = rms(middle)
    unit_two = middle * scale_two
    normed_own = (unit_two * gain_two).astype(BF16)
    ffn_pieces = both_cores(ffn_mine)
    normed_two = all_z(normed_own)

    d_two, d_gu, activation = ffn_block(
        normed_two, blocks, ffn_pieces
    )
    ffn_pairs = [
        ([(v, 0) for v in normed_two], d_gu),
        ([(v, 128) for v in blocks], activation),
    ]
    ffn_sent = grads_half(ffn_pairs, FF_PAD, "other")
    d_normed_two = sum_z(d_two)
    pulled = d_normed_two * gain_two
    d_middle = cotangent.astype(F32) + scale_two * (
        pulled - unit_two * jnp.mean(pulled * unit_two, axis=-1, keepdims=True)
    )
    gain_two_part = jnp.sum(d_normed_two * unit_two, axis=0)
    ffn_sent, d_mixer_own = together(ffn_sent, d_middle.astype(BF16))
    d_mixer_blocks = all_z(d_mixer_own)
    ffn_half = grads_half(ffn_pairs, FF_PAD, "own", other_core(ffn_sent))
    ffn_half, d_mixer_blocks = together(ffn_half, d_mixer_blocks)
    ffn_got = {m: second_axis(ffn_half[m], m) for m in (1, 3)}

    d_conv, d_c = mixer_pull(d_mixer_blocks, proj, conv, wout)
    d_conv, act_late = together(d_conv, activation)
    outside = from_group(lax.dynamic_slice_in_dim(d_conv, z * 128, 16, 0), 1)
    ffn = down_projection(act_late, ffn_pieces)
    outside, ffn, ffn_last = together(outside, ffn, ffn_half[2])
    ffn_got[2] = second_axis(ffn_last, 2)
    sent, d_projected, extra = mixer_backward(
        blocks, d_conv, d_c, outside, proj, prod, scale_one, taps, lengths, win,
        gain_two_part[None],
    )
    mixer_pairs = [
        ([(normed_one, 0)], d_projected),
        ([(v, 0) for v in d_mixer_blocks], gated),
    ]
    mixer_half = grads_half(mixer_pairs, 128, "both", extra)
    sent, mixer_half, ffn_got[1], ffn_got[3] = together(
        sent, mixer_half, ffn_got[1], ffn_got[3]
    )
    mixer_got = {m: second_axis(mixer_half[m], m) for m in (2, 1, 3)}
    d_normed_one = sum_z(sent)
    ffn, d_normed_one, ffn_got[2] = together(ffn, d_normed_one, ffn_got[2])
    ffn_out = sum_z(ffn)
    mixed = (middle + ffn_out).astype(BF16)
    ffn_total = second_sum(ffn_half[0], ffn_got)
    mixer_total = second_sum(mixer_half[0], mixer_got)
    small = mixer_total[256:261] + mixer_total[261:266]
    (mixer_both, ffn_grads), small = scatter_first(
        [mixer_total[:256].reshape(4, 64, 1024), ffn_total], small
    )
    small = small + other_core(small)
    small = small + sum(along_z(small, m) for m in (2, 1, 3))
    mixer_grads = mixer_both[:, :512] + other_core(mixer_both[:, 512:].astype(BF16)).astype(F32)

    scale_own = rms(residual)
    unit_one = residual * scale_own
    pulled_one = d_normed_one * gain_one
    grad_tokens = d_middle + scale_own * (
        pulled_one - unit_one * jnp.mean(pulled_one * unit_one, axis=-1, keepdims=True)
    )

    return (
        mixed,
        grad_tokens,
        small[0],
        mixer_grads[:, :384].reshape(64, 3, 128),
        small[2:],
        mixer_grads[:, 384:].T,
        small[1],
        jnp.stack([ffn_grads[:, :FF_BLOCK], ffn_grads[:, FF_PAD : FF_PAD + FF_BLOCK]]),
        ffn_grads[:, 2 * FF_PAD : 2 * FF_PAD + FF_BLOCK].T,
    )


def solution(mesh):
    fine = Mesh(mesh.devices.reshape(SIZES), AXES)
    rows = P(AXES, None)
    fsdp_ctx = ("x", "core", "ylo")
    tp = ("yhi", "z")
    return jax.shard_map(
        body,
        mesh=fine,
        in_specs=(
            rows,
            P(("x", "core"), None),
            P(),
            P(fsdp_ctx, None, tp),
            P(),
            P(tp, fsdp_ctx),
            P(),
            P(None, fsdp_ctx, tp),
            P(tp, fsdp_ctx),
            rows,
        ),
        out_specs=(
            rows,
            rows,
            P(),
            P(fsdp_ctx, None, tp),
            P(),
            P(tp, fsdp_ctx),
            P(),
            P(None, fsdp_ctx, tp),
            P(tp, fsdp_ctx),
        ),
        check_vma=False,
    )
```

```python
import jax
import jax.numpy as jnp
from jax import lax
from jax.experimental import pallas as pl
from jax.experimental.pallas import tpu as pltpu
from jax.sharding import Mesh
from jax.sharding import PartitionSpec as P

EPS = 1e-05
F32 = jnp.float32
BF16 = jnp.bfloat16
AXES = ("x", "core", "ylo", "yhi", "z")
SIZES = (4, 2, 2, 2, 4)
SPACE_ANY = pl.BlockSpec(memory_space=pl.ANY)
SPACE_VMEM = pl.BlockSpec(memory_space=pltpu.VMEM)
SPACE_SMEM = pl.BlockSpec(memory_space=pltpu.SMEM)
CONTRACT_LAST = (((1,), (1,)), ((), ()))
CONTRACT_FIRST = (((0,), (0,)), ((), ()))
FF_BLOCK = 576
FF_PAD = 640


def device_number(x, core, y, z):
    return (((x * 2 + core) * 2 + y % 2) * 2 + y // 2) * 4 + z


def route(step):
    return [
        (device_number(x, core, y, z), device_number(*step(x, core, y, z)))
        for x in range(4)
        for core in range(2)
        for y in range(4)
        for z in range(4)
    ]


def along_z(value, m):
    return lax.ppermute(value, AXES, route(lambda x, c, y, z: (x, c, y, z ^ m)))


def along_x(value, m):
    return lax.ppermute(value, AXES, route(lambda x, c, y, z: (x ^ m, c, y, z)))


def along_y(value, m):
    return lax.ppermute(value, AXES, route(lambda x, c, y, z: (x, c, y ^ m, z)))


def other_core(value):
    return lax.ppermute(value, AXES, route(lambda x, c, y, z: (x, 1 - c, y, z)))


def first_axis(value, m):
    def step(x, c, y, z):
        return (x ^ m, c, y, z) if c == 0 else (x, c, y ^ m, z)

    return lax.ppermute(value, AXES, route(step))


def second_axis(value, m):
    def step(x, c, y, z):
        return (x, c, y ^ m, z) if c == 0 else (x ^ m, c, y, z)

    return lax.ppermute(value, AXES, route(step))


def second_groups():
    groups = [
        [device_number(x, 0, y, z) for y in range(4)] for x in range(4) for z in range(4)
    ]
    return groups + [
        [device_number(x, 1, y, z) for x in range(4)] for y in range(4) for z in range(4)
    ]


def grouped_second(own):
    spread = jnp.broadcast_to(own[None], (4, *own.shape))
    return lax.all_to_all(spread, AXES, 0, 0, axis_index_groups=second_groups())


def together(*values):
    return lax.optimization_barrier(values)


def all_z(own):
    got = {m: along_z(own, m) for m in (2, 1, 3)}
    return [own, got[1], got[2], got[3]]


def sum_z(blocks):
    got = {m: along_z(blocks[m], m) for m in (2, 1, 3)}
    return sum(v.astype(F32) for v in (blocks[0], got[1], got[2], got[3]))


def all_first(own):
    got = {m: first_axis(own, m) for m in (2, 1, 3)}
    return [own, got[1], got[2], got[3]]


def all_second(own):
    got = {m: second_axis(own, m) for m in (2, 1, 3)}
    return [own, got[1], got[2], got[3]]


def both_cores(pieces):
    return [*pieces, other_core(pieces[0]), other_core(jnp.stack(pieces[1:]))]


def split_rows(vector, rows, width):
    high = lax.reduce_precision(vector, 8, 7)
    both = jnp.stack([high.astype(BF16), (vector - high).astype(BF16)]).reshape(-1, width)
    return jnp.pad(both, ((0, rows - both.shape[0]), (0, 0)))


def joined_rows(rows, shape):
    count = shape[0] * shape[1] // rows.shape[1]
    return (rows[:count] + rows[count : 2 * count]).reshape(shape)


def from_group(block, shift):
    pairs = []
    for x in range(4):
        for c in range(2):
            for y in range(4):
                for z in range(4):
                    to = (y % 2) * 2 + y // 2 - shift
                    if 0 <= to < 4:
                        target = device_number(x, c, (to % 2) * 2 + to // 2, z)
                        pairs.append((device_number(x, c, y, z), target))
    return lax.ppermute(block, AXES, pairs)


def position():
    y = lax.axis_index("yhi") * 2 + lax.axis_index("ylo")
    return lax.axis_index("x"), lax.axis_index("core"), y, lax.axis_index("z")


def first_token(m):
    _, _, y, z = position()
    return (((y % 2) * 2 + y // 2) * 4 + (z ^ m)) * 128


def weight_copies(pieces, targets, sems):
    x, core, y, _ = position()
    sources = [*pieces[:5], *(pieces[5].at[i] for i in range(3))]
    copies = []
    for ref, start, count, width in targets:
        for i in range(count):
            for p in range(8):
                k = core if p < 4 else 1 - core
                for m in range(4):
                    x_from = jnp.where(k == 0, x ^ m, x ^ (p % 4))
                    y_from = jnp.where(k == 0, y ^ (p % 4), y ^ m)
                    row = pl.multiple_of(((x_from * 2 + k) * 2 + y_from % 2) * 64, 64)
                    col = pl.multiple_of((i * 2 + y_from // 2) * width, 128)
                    copies.append(
                        pltpu.make_async_copy(
                            sources[p].at[m, :, pl.ds(start + i * width, width)],
                            ref.at[pl.ds(row, 64), pl.ds(col, width)],
                            sems.at[len(copies)],
                        )
                    )
    return copies


def grouped_copies(pieces, targets, sems):
    x, core, y, _ = position()
    copies = []
    for p in range(2):
        k = core if p == 0 else 1 - core
        for s in range(4):
            for m in range(4):
                x_from = jnp.where(k == 0, x ^ m, s)
                y_from = jnp.where(k == 0, s, y ^ m)
                row = pl.multiple_of(((x_from * 2 + k) * 2 + y_from % 2) * 64, 64)
                for ref, start, count, width in targets:
                    for i in range(count):
                        col = pl.multiple_of((i * 2 + y_from // 2) * width, 128)
                        copies.append(
                            pltpu.make_async_copy(
                                pieces[p].at[s, m, :, pl.ds(start + i * width, width)],
                                ref.at[pl.ds(row, 64), pl.ds(col, width)],
                                sems.at[len(copies)],
                            )
                        )
    return copies


def rms(values):
    return lax.rsqrt(jnp.mean(values * values, axis=-1, keepdims=True) + EPS)


def call(kernel, outs, in_specs, scratch, args, flops=0, traffic=0, vmem=14):
    return pl.pallas_call(
        kernel,
        out_shape=tuple(jax.ShapeDtypeStruct(shape, dtype) for shape, dtype in outs),
        in_specs=in_specs,
        out_specs=(SPACE_VMEM,) * len(outs),
        scratch_shapes=scratch,
        cost_estimate=pl.CostEstimate(flops=flops, bytes_accessed=traffic, transcendentals=0),
        compiler_params=pltpu.CompilerParams(vmem_limit_bytes=vmem * 2**20),
    )(*args)


def mixer_forward_kernel(*refs):
    blocks, behind, gain, taps, length = refs[:4], refs[4], refs[5], refs[6], refs[7]
    pieces = refs[8:10]
    parts = refs[10:14]
    normed, proj, conv, prod, scale, gated, win, wout = refs[14:22]
    wide, sems = refs[22:]
    _, _, _, z = position()
    copies = grouped_copies(pieces, ((win, 0, 3, 128), (wout, 384, 1, 128)), sems)
    for c in copies:
        c.start()

    def scaled(values):
        return (values * rms(values) * gain[...]).astype(BF16)

    for m in range(4):
        values = blocks[m][:128, :].astype(F32)
        inverse = rms(values)
        rows = (values * inverse * gain[...]).astype(BF16)
        wide[m * 144 + 16 : (m + 1) * 144, :] = rows
        normed[m * 128 : (m + 1) * 128, :] = rows
        scale[m * 128 : (m + 1) * 128, :] = inverse
    outside = scaled(behind[...].astype(F32))
    for m in range(4):
        here = z ^ m
        at = pl.multiple_of(((here + 3) % 4 ^ z) * 128 + 112, 16)
        wide[m * 144 : m * 144 + 16, :] = jnp.where(here > 0, normed[pl.ds(at, 16), :], outside)
    for c in copies:
        c.wait()
    out = jnp.dot(wide[...], win[...], preferred_element_type=F32)
    for m in range(4):
        rows = slice(m * 128, (m + 1) * 128)
        here = out[m * 144 : (m + 1) * 144]
        proj[rows, :] = here[16:]
        product = (here[:, :256] * here[:, 512:]).astype(BF16).astype(F32)
        prod[m] = product
        places = first_token(m) + lax.broadcasted_iota(jnp.int32, (128, 256), 0)
        live = places < length[0, 0]
        one = jnp.where((places >= 1) & live, 1.0, 0.0)
        two = jnp.where((places >= 2) & live, 1.0, 0.0)
        conv_out = (
            taps[2:3, :] * product[16:]
            + one * (taps[1:2, :] * product[15:143])
            + two * (taps[0:1, :] * product[14:142])
        )
        conv[rows, :] = conv_out
        gated[rows, :] = (here[16:, 256:512] * conv_out).astype(BF16)
    out = lax.dot_general(gated[...], wout[...], CONTRACT_LAST, preferred_element_type=F32)
    for m in range(4):
        parts[m][...] = out[m * 128 : (m + 1) * 128].astype(BF16)


def mixer_forward(blocks, behind, gain, taps, length, pieces):
    out = call(
        mixer_forward_kernel,
        (
            *[((128, 1024), BF16)] * 4,
            ((512, 1024), BF16),
            ((512, 768), F32),
            ((512, 256), F32),
            ((4, 144, 256), F32),
            ((512, 1), F32),
            ((512, 256), BF16),
            ((1024, 768), BF16),
            ((1024, 256), BF16),
        ),
        [SPACE_VMEM] * 7 + [SPACE_SMEM] + [SPACE_ANY] * 2,
        [pltpu.VMEM((576, 1024), BF16), pltpu.SemaphoreType.DMA((128,))],
        (*blocks, behind, gain, taps, length, *pieces),
        flops=2 * 576 * 1024 * 1024,
        traffic=2**23,
        vmem=24,
    )
    return out[:4], *out[4:]


def ffn_kernel(*refs):
    n_blocks, c_blocks, pieces = refs[:4], refs[4:8], refs[8:14]
    d_two, d_gu, act = refs[14:18], refs[18], refs[19]
    weights, normed, cot, sems = refs[20:]
    copies = weight_copies(pieces, ((weights, 0, 3, FF_PAD),), sems)
    for c in copies:
        c.start()
    for m in range(4):
        normed[m * 128 : (m + 1) * 128, :] = n_blocks[m][...]
        cot[m * 128 : (m + 1) * 128, :] = c_blocks[m][128:, :]
    wide = 2 * FF_PAD
    results = []
    for i, left in enumerate((normed, normed, cot)):
        for c in copies[i * 32 : (i + 1) * 32]:
            c.wait()
        cols = slice(i * wide, (i + 1) * wide)
        results.append(jnp.dot(left[...], weights[:, cols], preferred_element_type=F32))
    gate, up, da = results
    sig = jax.nn.sigmoid(gate)
    swish = gate * sig
    d_gate = (da * up * sig * (1.0 + gate * (1.0 - sig))).astype(BF16)
    d_up = (da * swish).astype(BF16)
    act[...] = (swish * up).astype(BF16)
    d_gu[:, :wide] = d_gate
    d_gu[:, wide:] = d_up
    total = lax.dot_general(
        d_gu[...], weights[:, : 2 * wide], CONTRACT_LAST, preferred_element_type=F32
    )
    for m in range(4):
        d_two[m][...] = total[m * 128 : (m + 1) * 128, :].astype(BF16)


def ffn_block(n_blocks, c_blocks, pieces):
    out = call(
        ffn_kernel,
        (
            *[((128, 1024), BF16)] * 4,
            ((512, 4 * FF_PAD), BF16),
            ((512, 2 * FF_PAD), BF16),
        ),
        [SPACE_VMEM] * 8 + [SPACE_ANY] * 6,
        [
            pltpu.VMEM((1024, 6 * FF_PAD), BF16),
            pltpu.VMEM((512, 1024), BF16),
            pltpu.VMEM((512, 1024), BF16),
            pltpu.SemaphoreType.DMA((96,)),
        ],
        (*n_blocks, *c_blocks, *pieces),
        flops=2 * 512 * 1024 * 6 * FF_PAD * 2,
        traffic=2**24,
        vmem=40,
    )
    return out[:4], *out[4:]


def down_kernel(*refs):
    act, pieces, outs = refs[0], refs[1:7], refs[7:11]
    weights, sems = refs[11:]
    copies = weight_copies(pieces, ((weights, 2 * FF_PAD, 1, FF_PAD),), sems)
    for c in copies:
        c.start()
    for c in copies:
        c.wait()
    product = lax.dot_general(act[...], weights[...], CONTRACT_LAST, preferred_element_type=F32)
    for m in range(4):
        outs[m][...] = product[m * 128 : (m + 1) * 128].astype(BF16)


def down_projection(act, pieces):
    return call(
        down_kernel,
        (((128, 1024), BF16),) * 4,
        [SPACE_VMEM] + [SPACE_ANY] * 6,
        [pltpu.VMEM((1024, 2 * FF_PAD), BF16), pltpu.SemaphoreType.DMA((32,))],
        (act, *pieces),
        flops=2 * 512 * 1024 * 2 * FF_PAD,
        traffic=2**22,
    )


def grads_kernel(mode, width, pairs, *refs):
    received = None if mode == "other" else refs[0]
    outs, turned, full = refs[-6:-2], refs[-2], refs[-1]
    x, core, y, _ = position()
    carrier = 1 - core if mode == "other" else core
    owners = (core, 1 - core) if mode == "both" else (carrier,)
    at = 0
    for lefts, right in pairs:
        for b, owner in enumerate(owners):
            for x_to in range(4):
                lanes = pl.ds(pl.multiple_of((x_to * 2 + owner) * 128, 128), 128)
                first = b * 512 + x_to * 128
                token = 0
                for left, skip in lefts:
                    count = left.shape[0] - skip
                    turned[first : first + 128, token : token + count] = left[skip:, lanes].T
                    token += count
        for i in range(right.shape[1] // (2 * width)):
            full[:, at : at + 2 * width] = jnp.dot(
                turned[...],
                right[:, i * 2 * width : (i + 1) * 2 * width],
                preferred_element_type=F32,
            ).astype(BF16)
            at += 2 * width
    count = at // (2 * width)
    for s in range(4):
        for f in range(4):
            x_to = x ^ jnp.where(carrier == 0, f, s)
            y_to = y ^ jnp.where(carrier == 0, s, f)
            for b in range(len(owners)):
                rows = pl.ds(pl.multiple_of(b * 512 + x_to * 128 + (y_to % 2) * 64, 64), 64)
                for i in range(count):
                    cols = pl.ds(pl.multiple_of((i * 2 + y_to // 2) * width, 128), width)
                    here = slice((b * count + i) * width, (b * count + i + 1) * width)
                    piece = full[rows, cols]
                    if mode == "own":
                        piece = (piece.astype(F32) + received[s, f, :, here].astype(F32)).astype(BF16)
                    if mode == "other":
                        outs[0][s, f, :, here] = piece
                    elif mode == "own":
                        outs[s][f, :, here] = piece
                    else:
                        outs[s][f * 64 : (f + 1) * 64, here] = piece
        if mode == "both":
            outs[s][256:, :] = received[...]


def grads_half(pairs, width, mode, received=None):
    total = sum(right.shape[1] for _, right in pairs) // 2
    cores = 2 if mode == "both" else 1
    args = [v for lefts, right in pairs for v in (*(left for left, _ in lefts), right)]

    def kernel(*refs):
        given, at = [], 0
        for lefts, _ in pairs:
            count = len(lefts)
            skips = [skip for _, skip in lefts]
            given.append((list(zip(refs[at : at + count], skips)), refs[at + count]))
            at += count + 1
        rest = refs[at:]
        if mode == "other":
            rest = (rest[0], None, None, None, *rest[1:])
        grads_kernel(mode, width, given, *rest)

    out = call(
        kernel,
        {
            "other": (((4, 4, 64, total), BF16),),
            "own": (((4, 64, total), BF16),) * 4,
            "both": (((272, 2 * total), BF16),) * 4,
        }[mode],
        [SPACE_VMEM] * (len(args) + (mode != "other")),
        [pltpu.VMEM((cores * 512, 512), BF16), pltpu.VMEM((cores * 512, 2 * total), BF16)],
        (*args, *(() if mode == "other" else (received,))),
        flops=2 * 512 * 512 * total * 2,
        traffic=2**23,
        vmem=16,
    )
    return out[0] if mode == "other" else out


def second_sum(own, got):
    return sum(v.astype(F32) for v in (own, got[1], got[2], got[3]))


def scatter_first(parts, small=None):
    width = sum(p.shape[2] for p in parts)
    extra = [] if small is None else [split_rows(small, 64, 256)]
    last = {
        m: first_axis(jnp.concatenate([*(p[m].astype(BF16) for p in parts), *extra], axis=1), m)
        for m in (2, 1, 3)
    }
    came = sum(last[m].astype(F32) for m in (1, 2, 3))
    out, at = [], 0
    for p in parts:
        out.append(p[0] + came[:, at : at + p.shape[2]])
        at += p.shape[2]
    if small is None:
        return out
    return out, small + joined_rows(came[:, width:], small.shape)


def mixer_pull_kernel(*refs):
    blocks, proj, conv, wout = refs[:4], refs[4], refs[5], refs[6]
    d_conv, d_c, d_mixer = refs[7:]
    for m in range(4):
        d_mixer[m * 128 : (m + 1) * 128, :] = blocks[m][...]
    d_gated = jnp.dot(d_mixer[...], wout[...], preferred_element_type=F32)
    d_conv[...] = (d_gated * proj[:, 256:512]).astype(BF16)
    d_c[...] = (d_gated * conv[...]).astype(BF16)


def mixer_pull(blocks, proj, conv, wout):
    return call(
        mixer_pull_kernel,
        (((512, 256), BF16), ((512, 256), BF16)),
        [SPACE_VMEM] * 7,
        [pltpu.VMEM((512, 1024), BF16)],
        (*blocks, proj, conv, wout),
        flops=2 * 512 * 1024 * 256,
        traffic=2**21,
        vmem=8,
    )


def mixer_backward_kernel(*refs):
    blocks = refs[:4]
    d_conv, d_c, outside, proj, prod, scale, taps, length, win, gain_two = refs[4:14]
    sent = refs[14:18]
    d_proj, extra, small = refs[18:]
    _, _, _, z = position()
    small[...] = jnp.zeros((5, 1024), F32)
    sums = [0.0, 0.0, 0.0]
    for m in range(4):
        here = z ^ m
        rows = slice(m * 128, (m + 1) * 128)
        at = pl.multiple_of(((here + 1) % 4 ^ z) * 128, 128)
        inner = d_conv[pl.ds(at, 16), :].astype(F32)
        following = jnp.where(here < 3, inner, outside[...].astype(F32))
        places = first_token(m) + lax.broadcasted_iota(jnp.int32, (128, 256), 0)
        live = places < length[0, 0]
        one = jnp.where((places >= 1) & live, 1.0, 0.0)
        two = jnp.where((places >= 2) & live, 1.0, 0.0)
        one_back = jnp.where(places + 1 < length[0, 0], 1.0, 0.0)
        two_back = jnp.where(places + 2 < length[0, 0], 1.0, 0.0)
        pull = d_conv[rows, :].astype(F32)
        longer = jnp.concatenate([pull, following], axis=0)
        d_product = (
            taps[2:3, :] * pull
            + one_back * (taps[1:2, :] * longer[1:129])
            + two_back * (taps[0:1, :] * longer[2:130])
        )
        d_proj[rows, :256] = (d_product * proj[rows, 512:]).astype(BF16)
        d_proj[rows, 256:512] = d_c[rows, :]
        d_proj[rows, 512:] = (d_product * proj[rows, :256]).astype(BF16)
        sums[0] += jnp.sum(pull * two * prod[m, 14:142, :], axis=0, keepdims=True)
        sums[1] += jnp.sum(pull * one * prod[m, 15:143, :], axis=0, keepdims=True)
        sums[2] += jnp.sum(pull * prod[m, 16:, :], axis=0, keepdims=True)
    for h in range(2):
        lanes = pl.ds(pl.multiple_of((h * 4 + z) * 128, 128), 128)
        for i in range(3):
            small[2 + i : 3 + i, lanes] = sums[i][:, h * 128 : (h + 1) * 128]
    out = lax.dot_general(d_proj[...], win[...], CONTRACT_LAST, preferred_element_type=F32)
    gain = 0.0
    for m in range(4):
        rows = slice(m * 128, (m + 1) * 128)
        unit = blocks[m][:128, :].astype(F32) * scale[rows, :]
        gain += jnp.sum(out[rows] * unit, axis=0, keepdims=True)
        sent[m][...] = out[rows].astype(BF16)
    small[0:1, :] = gain
    small[1:2, :] = gain_two[...]
    high = small[...].astype(BF16)
    low = (small[...] - high.astype(F32)).astype(BF16)
    rows = jnp.concatenate([high.astype(F32), low.astype(F32), jnp.zeros((6, 1024), F32)], axis=0)
    extra[...] = rows.astype(BF16)


def mixer_backward(
    blocks, d_conv, d_c, outside, proj, prod, scale, taps, length, win, gain_two
):
    out = call(
        mixer_backward_kernel,
        (
            *[((128, 1024), BF16)] * 4,
            ((512, 768), BF16),
            ((16, 1024), BF16),
        ),
        [SPACE_VMEM] * 11 + [SPACE_SMEM] + [SPACE_VMEM] * 2,
        [pltpu.VMEM((5, 1024), F32)],
        (*blocks, d_conv, d_c, outside, proj, prod, scale, taps, length, win, gain_two),
        flops=2 * 512 * 1024 * 768,
        traffic=2**23,
    )
    return out[:4], out[4], out[5]


def body(tokens, lengths, gain_one, w_in, conv_weight, w_out, gain_two, w_gu, w_down, cotangent):
    z = lax.axis_index("z")
    tail = jnp.zeros((64, FF_PAD - FF_BLOCK), BF16)
    pack = jnp.concatenate(
        [w_in[:, 0], w_in[:, 1], w_in[:, 2], w_out.T]
        + [w_gu[0], tail, w_gu[1], tail, w_down.T, tail],
        axis=1,
    )
    first = all_first(pack)
    blocks = all_z(jnp.concatenate([tokens, cotangent], axis=0))
    mixer_mine = grouped_second(jnp.stack([v[:, :512] for v in first]))
    ends = jnp.stack([v[112:128] for v in blocks])
    behind = from_group(lax.dynamic_index_in_dim(ends, 3 ^ z, 0, keepdims=False), -1)
    mixer_mine, ffn_first = together(mixer_mine, jnp.stack([v[:, 512:] for v in first]))
    mixer_pieces = (mixer_mine, other_core(mixer_mine))
    ffn_got = {m: second_axis(ffn_first, m) for m in (1, 3)}
    behind, ffn_late = together(behind, ffn_first)
    ffn_got[2] = second_axis(ffn_late, 2)
    taps = jnp.concatenate(
        [
            lax.dynamic_slice_in_dim(conv_weight, z * 128, 128, 1),
            lax.dynamic_slice_in_dim(conv_weight, 512 + z * 128, 128, 1),
        ],
        axis=1,
    )
    residual = tokens.astype(F32)

    part, normed_one, proj, conv, prod, scale_one, gated, win, wout = mixer_forward(
        blocks, behind, gain_one[None], taps, lengths, mixer_pieces
    )
    middle = residual + sum_z(part)
    ffn_got, middle = together(ffn_got, middle)
    ffn_mine = [ffn_first, ffn_got[1], ffn_got[2], ffn_got[3]]
    scale_two = rms(middle)
    unit_two = middle * scale_two
    normed_own = (unit_two * gain_two).astype(BF16)
    ffn_pieces = both_cores(ffn_mine)
    normed_two = all_z(normed_own)

    d_two, d_gu, activation = ffn_block(
        normed_two, blocks, ffn_pieces
    )
    ffn_pairs = [
        ([(v, 0) for v in normed_two], d_gu),
        ([(v, 128) for v in blocks], activation),
    ]
    ffn_sent = grads_half(ffn_pairs, FF_PAD, "other")
    d_normed_two = sum_z(d_two)
    pulled = d_normed_two * gain_two
    d_middle = cotangent.astype(F32) + scale_two * (
        pulled - unit_two * jnp.mean(pulled * unit_two, axis=-1, keepdims=True)
    )
    gain_two_part = jnp.sum(d_normed_two * unit_two, axis=0)
    ffn_sent, d_mixer_own = together(ffn_sent, d_middle.astype(BF16))
    d_mixer_blocks = all_z(d_mixer_own)
    ffn_half = grads_half(ffn_pairs, FF_PAD, "own", other_core(ffn_sent))
    ffn_half, d_mixer_blocks = together(ffn_half, d_mixer_blocks)
    ffn_got = {m: second_axis(ffn_half[m], m) for m in (1, 3)}

    d_conv, d_c = mixer_pull(d_mixer_blocks, proj, conv, wout)
    d_conv, act_late = together(d_conv, activation)
    outside = from_group(lax.dynamic_slice_in_dim(d_conv, z * 128, 16, 0), 1)
    ffn = down_projection(act_late, ffn_pieces)
    outside, ffn, ffn_last = together(outside, ffn, ffn_half[2])
    ffn_got[2] = second_axis(ffn_last, 2)
    sent, d_projected, extra = mixer_backward(
        blocks, d_conv, d_c, outside, proj, prod, scale_one, taps, lengths, win,
        gain_two_part[None],
    )
    mixer_pairs = [
        ([(normed_one, 0)], d_projected),
        ([(v, 0) for v in d_mixer_blocks], gated),
    ]
    mixer_half = grads_half(mixer_pairs, 128, "both", extra)
    sent, mixer_half, ffn_got[1], ffn_got[3] = together(
        sent, mixer_half, ffn_got[1], ffn_got[3]
    )
    mixer_got = {m: second_axis(mixer_half[m], m) for m in (2, 1, 3)}
    d_normed_one = sum_z(sent)
    ffn, d_normed_one, ffn_got[2] = together(ffn, d_normed_one, ffn_got[2])
    ffn_out = sum_z(ffn)
    mixed = (middle + ffn_out).astype(BF16)
    ffn_total = second_sum(ffn_half[0], ffn_got)
    mixer_total = second_sum(mixer_half[0], mixer_got)
    small = mixer_total[256:261] + mixer_total[261:266]
    (mixer_both, ffn_grads), small = scatter_first(
        [mixer_total[:256].reshape(4, 64, 1024), ffn_total], small
    )
    small = small + other_core(small)
    small = small + sum(along_z(small, m) for m in (2, 1, 3))
    mixer_grads = mixer_both[:, :512] + other_core(mixer_both[:, 512:].astype(BF16)).astype(F32)

    scale_own = rms(residual)
    unit_one = residual * scale_own
    pulled_one = d_normed_one * gain_one
    grad_tokens = d_middle + scale_own * (
        pulled_one - unit_one * jnp.mean(pulled_one * unit_one, axis=-1, keepdims=True)
    )

    return (
        mixed,
        grad_tokens,
        small[0],
        mixer_grads[:, :384].reshape(64, 3, 128),
        small[2:],
        mixer_grads[:, 384:].T,
        small[1],
        jnp.stack([ffn_grads[:, :FF_BLOCK], ffn_grads[:, FF_PAD : FF_PAD + FF_BLOCK]]),
        ffn_grads[:, 2 * FF_PAD : 2 * FF_PAD + FF_BLOCK].T,
    )


def solution(mesh):
    fine = Mesh(mesh.devices.reshape(SIZES), AXES)
    rows = P(AXES, None)
    fsdp_ctx = ("x", "core", "ylo")
    tp = ("yhi", "z")
    return jax.shard_map(
        body,
        mesh=fine,
        in_specs=(
            rows,
            P(("x", "core"), None),
            P(),
            P(fsdp_ctx, None, tp),
            P(),
            P(tp, fsdp_ctx),
            P(),
            P(None, fsdp_ctx, tp),
            P(tp, fsdp_ctx),
            rows,
        ),
        out_specs=(
            rows,
            rows,
            P(),
            P(fsdp_ctx, None, tp),
            P(),
            P(tp, fsdp_ctx),
            P(),
            P(None, fsdp_ctx, tp),
            P(tp, fsdp_ctx),
        ),
        check_vma=False,
    )
```

```python
import jax
import jax.numpy as jnp
from jax import lax
from jax.experimental import pallas as pl
from jax.experimental.pallas import tpu as pltpu
from jax.sharding import Mesh
from jax.sharding import PartitionSpec as P

EPS = 1e-05
F32 = jnp.float32
BF16 = jnp.bfloat16
AXES = ("x", "core", "ylo", "yhi", "z")
SIZES = (4, 2, 2, 2, 4)
SPACE_ANY = pl.BlockSpec(memory_space=pl.ANY)
SPACE_VMEM = pl.BlockSpec(memory_space=pltpu.VMEM)
SPACE_SMEM = pl.BlockSpec(memory_space=pltpu.SMEM)
CONTRACT_LAST = (((1,), (1,)), ((), ()))
CONTRACT_FIRST = (((0,), (0,)), ((), ()))
FF_BLOCK = 576
FF_PAD = 640


def device_number(x, core, y, z):
    return (((x * 2 + core) * 2 + y % 2) * 2 + y // 2) * 4 + z


def route(step):
    return [
        (device_number(x, core, y, z), device_number(*step(x, core, y, z)))
        for x in range(4)
        for core in range(2)
        for y in range(4)
        for z in range(4)
    ]


def along_z(value, m):
    return lax.ppermute(value, AXES, route(lambda x, c, y, z: (x, c, y, z ^ m)))


def along_x(value, m):
    return lax.ppermute(value, AXES, route(lambda x, c, y, z: (x ^ m, c, y, z)))


def along_y(value, m):
    return lax.ppermute(value, AXES, route(lambda x, c, y, z: (x, c, y ^ m, z)))


def other_core(value):
    return lax.ppermute(value, AXES, route(lambda x, c, y, z: (x, 1 - c, y, z)))


def first_axis(value, m):
    def step(x, c, y, z):
        return (x ^ m, c, y, z) if c == 0 else (x, c, y ^ m, z)

    return lax.ppermute(value, AXES, route(step))


def second_axis(value, m):
    def step(x, c, y, z):
        return (x, c, y ^ m, z) if c == 0 else (x ^ m, c, y, z)

    return lax.ppermute(value, AXES, route(step))


def second_groups():
    groups = [
        [device_number(x, 0, y, z) for y in range(4)] for x in range(4) for z in range(4)
    ]
    return groups + [
        [device_number(x, 1, y, z) for x in range(4)] for y in range(4) for z in range(4)
    ]


def grouped_second(own):
    spread = jnp.broadcast_to(own[None], (4, *own.shape))
    return lax.all_to_all(spread, AXES, 0, 0, axis_index_groups=second_groups())


def together(*values):
    return lax.optimization_barrier(values)


def all_z(own):
    got = {m: along_z(own, m) for m in (2, 1, 3)}
    return [own, got[1], got[2], got[3]]


def sum_z(blocks):
    got = {m: along_z(blocks[m], m) for m in (2, 1, 3)}
    return sum(v.astype(F32) for v in (blocks[0], got[1], got[2], got[3]))


def all_first(own):
    got = {m: first_axis(own, m) for m in (2, 1, 3)}
    return [own, got[1], got[2], got[3]]


def all_second(own):
    got = {m: second_axis(own, m) for m in (2, 1, 3)}
    return [own, got[1], got[2], got[3]]


def both_cores(pieces):
    return [*pieces, other_core(pieces[0]), other_core(jnp.stack(pieces[1:]))]


def split_rows(vector, rows, width):
    high = lax.reduce_precision(vector, 8, 7)
    both = jnp.stack([high.astype(BF16), (vector - high).astype(BF16)]).reshape(-1, width)
    return jnp.pad(both, ((0, rows - both.shape[0]), (0, 0)))


def joined_rows(rows, shape):
    count = shape[0] * shape[1] // rows.shape[1]
    return (rows[:count] + rows[count : 2 * count]).reshape(shape)


def from_group(block, shift):
    pairs = []
    for x in range(4):
        for c in range(2):
            for y in range(4):
                for z in range(4):
                    to = (y % 2) * 2 + y // 2 - shift
                    if 0 <= to < 4:
                        target = device_number(x, c, (to % 2) * 2 + to // 2, z)
                        pairs.append((device_number(x, c, y, z), target))
    return lax.ppermute(block, AXES, pairs)


def position():
    y = lax.axis_index("yhi") * 2 + lax.axis_index("ylo")
    return lax.axis_index("x"), lax.axis_index("core"), y, lax.axis_index("z")


def first_token(m):
    _, _, y, z = position()
    return (((y % 2) * 2 + y // 2) * 4 + (z ^ m)) * 128


def weight_copies(pieces, targets, sems):
    x, core, y, _ = position()
    sources = [*pieces[:5], *(pieces[5].at[i] for i in range(3))]
    copies = []
    for ref, start, count, width in targets:
        for i in range(count):
            for p in range(8):
                k = core if p < 4 else 1 - core
                for m in range(4):
                    x_from = jnp.where(k == 0, x ^ m, x ^ (p % 4))
                    y_from = jnp.where(k == 0, y ^ (p % 4), y ^ m)
                    row = pl.multiple_of(((x_from * 2 + k) * 2 + y_from % 2) * 64, 64)
                    col = pl.multiple_of((i * 2 + y_from // 2) * width, 128)
                    copies.append(
                        pltpu.make_async_copy(
                            sources[p].at[m, :, pl.ds(start + i * width, width)],
                            ref.at[pl.ds(row, 64), pl.ds(col, width)],
                            sems.at[len(copies)],
                        )
                    )
    return copies


def grouped_copies(pieces, targets, sems):
    x, core, y, _ = position()
    copies = []
    for p in range(2):
        k = core if p == 0 else 1 - core
        for s in range(4):
            for m in range(4):
                x_from = jnp.where(k == 0, x ^ m, s)
                y_from = jnp.where(k == 0, s, y ^ m)
                row = pl.multiple_of(((x_from * 2 + k) * 2 + y_from % 2) * 64, 64)
                for ref, start, count, width in targets:
                    for i in range(count):
                        col = pl.multiple_of((i * 2 + y_from // 2) * width, 128)
                        copies.append(
                            pltpu.make_async_copy(
                                pieces[p].at[s, m, :, pl.ds(start + i * width, width)],
                                ref.at[pl.ds(row, 64), pl.ds(col, width)],
                                sems.at[len(copies)],
                            )
                        )
    return copies


def rms(values):
    return lax.rsqrt(jnp.mean(values * values, axis=-1, keepdims=True) + EPS)


def call(kernel, outs, in_specs, scratch, args, flops=0, traffic=0, vmem=14):
    return pl.pallas_call(
        kernel,
        out_shape=tuple(jax.ShapeDtypeStruct(shape, dtype) for shape, dtype in outs),
        in_specs=in_specs,
        out_specs=(SPACE_VMEM,) * len(outs),
        scratch_shapes=scratch,
        cost_estimate=pl.CostEstimate(flops=flops, bytes_accessed=traffic, transcendentals=0),
        compiler_params=pltpu.CompilerParams(vmem_limit_bytes=vmem * 2**20),
    )(*args)


def mixer_forward_kernel(*refs):
    blocks, behind, gain, taps, length = refs[:4], refs[4], refs[5], refs[6], refs[7]
    pieces = refs[8:10]
    parts = refs[10:14]
    normed, proj, conv, prod, scale, gated, win, wout = refs[14:22]
    wide, sems = refs[22:]
    _, _, _, z = position()
    copies = grouped_copies(pieces, ((win, 0, 3, 128), (wout, 384, 1, 128)), sems)
    for c in copies:
        c.start()

    def scaled(values):
        return (values * rms(values) * gain[...]).astype(BF16)

    for m in range(4):
        values = blocks[m][:128, :].astype(F32)
        inverse = rms(values)
        rows = (values * inverse * gain[...]).astype(BF16)
        wide[m * 144 + 16 : (m + 1) * 144, :] = rows
        normed[m * 128 : (m + 1) * 128, :] = rows
        scale[m * 128 : (m + 1) * 128, :] = inverse
    outside = scaled(behind[...].astype(F32))
    for m in range(4):
        here = z ^ m
        at = pl.multiple_of(((here + 3) % 4 ^ z) * 128 + 112, 16)
        wide[m * 144 : m * 144 + 16, :] = jnp.where(here > 0, normed[pl.ds(at, 16), :], outside)
    for c in copies:
        c.wait()
    out = jnp.dot(wide[...], win[...], preferred_element_type=F32)
    for m in range(4):
        rows = slice(m * 128, (m + 1) * 128)
        here = out[m * 144 : (m + 1) * 144]
        proj[rows, :] = here[16:]
        product = (here[:, :256] * here[:, 512:]).astype(BF16).astype(F32)
        prod[m] = product
        places = first_token(m) + lax.broadcasted_iota(jnp.int32, (128, 256), 0)
        live = places < length[0, 0]
        one = jnp.where((places >= 1) & live, 1.0, 0.0)
        two = jnp.where((places >= 2) & live, 1.0, 0.0)
        conv_out = (
            taps[2:3, :] * product[16:]
            + one * (taps[1:2, :] * product[15:143])
            + two * (taps[0:1, :] * product[14:142])
        )
        conv[rows, :] = conv_out
        gated[rows, :] = (here[16:, 256:512] * conv_out).astype(BF16)
    out = lax.dot_general(gated[...], wout[...], CONTRACT_LAST, preferred_element_type=F32)
    for m in range(4):
        parts[m][...] = out[m * 128 : (m + 1) * 128].astype(BF16)


def mixer_forward(blocks, behind, gain, taps, length, pieces):
    out = call(
        mixer_forward_kernel,
        (
            *[((128, 1024), BF16)] * 4,
            ((512, 1024), BF16),
            ((512, 768), F32),
            ((512, 256), F32),
            ((4, 144, 256), F32),
            ((512, 1), F32),
            ((512, 256), BF16),
            ((1024, 768), BF16),
            ((1024, 256), BF16),
        ),
        [SPACE_VMEM] * 7 + [SPACE_SMEM] + [SPACE_ANY] * 2,
        [pltpu.VMEM((576, 1024), BF16), pltpu.SemaphoreType.DMA((128,))],
        (*blocks, behind, gain, taps, length, *pieces),
        flops=2 * 576 * 1024 * 1024,
        traffic=2**23,
        vmem=24,
    )
    return out[:4], *out[4:]


def ffn_kernel(*refs):
    n_blocks, c_blocks, pieces = refs[:4], refs[4:8], refs[8:14]
    d_two, d_gu, act = refs[14:18], refs[18], refs[19]
    weights, normed, cot, sems = refs[20:]
    copies = weight_copies(pieces, ((weights, 0, 3, FF_PAD),), sems)
    for c in copies:
        c.start()
    for m in range(4):
        normed[m * 128 : (m + 1) * 128, :] = n_blocks[m][...]
        cot[m * 128 : (m + 1) * 128, :] = c_blocks[m][128:, :]
    wide = 2 * FF_PAD
    results = []
    for i, left in enumerate((normed, normed, cot)):
        for c in copies[i * 32 : (i + 1) * 32]:
            c.wait()
        cols = slice(i * wide, (i + 1) * wide)
        results.append(jnp.dot(left[...], weights[:, cols], preferred_element_type=F32))
    gate, up, da = results
    sig = jax.nn.sigmoid(gate)
    swish = gate * sig
    d_gate = (da * up * sig * (1.0 + gate * (1.0 - sig))).astype(BF16)
    d_up = (da * swish).astype(BF16)
    act[...] = (swish * up).astype(BF16)
    d_gu[:, :wide] = d_gate
    d_gu[:, wide:] = d_up
    total = lax.dot_general(
        d_gu[...], weights[:, : 2 * wide], CONTRACT_LAST, preferred_element_type=F32
    )
    for m in range(4):
        d_two[m][...] = total[m * 128 : (m + 1) * 128, :].astype(BF16)


def ffn_block(n_blocks, c_blocks, pieces):
    out = call(
        ffn_kernel,
        (
            *[((128, 1024), BF16)] * 4,
            ((512, 4 * FF_PAD), BF16),
            ((512, 2 * FF_PAD), BF16),
        ),
        [SPACE_VMEM] * 8 + [SPACE_ANY] * 6,
        [
            pltpu.VMEM((1024, 6 * FF_PAD), BF16),
            pltpu.VMEM((512, 1024), BF16),
            pltpu.VMEM((512, 1024), BF16),
            pltpu.SemaphoreType.DMA((96,)),
        ],
        (*n_blocks, *c_blocks, *pieces),
        flops=2 * 512 * 1024 * 6 * FF_PAD * 2,
        traffic=2**24,
        vmem=40,
    )
    return out[:4], *out[4:]


def down_kernel(*refs):
    act, pieces, outs = refs[0], refs[1:7], refs[7:11]
    weights, sems = refs[11:]
    copies = weight_copies(pieces, ((weights, 2 * FF_PAD, 1, FF_PAD),), sems)
    for c in copies:
        c.start()
    for c in copies:
        c.wait()
    product = lax.dot_general(act[...], weights[...], CONTRACT_LAST, preferred_element_type=F32)
    for m in range(4):
        outs[m][...] = product[m * 128 : (m + 1) * 128].astype(BF16)


def down_projection(act, pieces):
    return call(
        down_kernel,
        (((128, 1024), BF16),) * 4,
        [SPACE_VMEM] + [SPACE_ANY] * 6,
        [pltpu.VMEM((1024, 2 * FF_PAD), BF16), pltpu.SemaphoreType.DMA((32,))],
        (act, *pieces),
        flops=2 * 512 * 1024 * 2 * FF_PAD,
        traffic=2**22,
    )


def grads_kernel(mode, width, pairs, *refs):
    received = None if mode == "other" else refs[0]
    outs, turned, full = refs[-6:-2], refs[-2], refs[-1]
    x, core, y, _ = position()
    carrier = 1 - core if mode == "other" else core
    owners = (core, 1 - core) if mode == "both" else (carrier,)
    at = 0
    for lefts, right in pairs:
        for b, owner in enumerate(owners):
            for x_to in range(4):
                lanes = pl.ds(pl.multiple_of((x_to * 2 + owner) * 128, 128), 128)
                first = b * 512 + x_to * 128
                token = 0
                for left, skip in lefts:
                    count = left.shape[0] - skip
                    turned[first : first + 128, token : token + count] = left[skip:, lanes].T
                    token += count
        for i in range(right.shape[1] // (2 * width)):
            full[:, at : at + 2 * width] = jnp.dot(
                turned[...],
                right[:, i * 2 * width : (i + 1) * 2 * width],
                preferred_element_type=F32,
            ).astype(BF16)
            at += 2 * width
    count = at // (2 * width)
    for s in range(4):
        for f in range(4):
            x_to = x ^ jnp.where(carrier == 0, f, s)
            y_to = y ^ jnp.where(carrier == 0, s, f)
            for b in range(len(owners)):
                rows = pl.ds(pl.multiple_of(b * 512 + x_to * 128 + (y_to % 2) * 64, 64), 64)
                for i in range(count):
                    cols = pl.ds(pl.multiple_of((i * 2 + y_to // 2) * width, 128), width)
                    here = slice((b * count + i) * width, (b * count + i + 1) * width)
                    piece = full[rows, cols]
                    if mode == "own":
                        piece = (piece.astype(F32) + received[s, f, :, here].astype(F32)).astype(BF16)
                    if mode == "other":
                        outs[0][s, f, :, here] = piece
                    elif mode == "own":
                        outs[s][f, :, here] = piece
                    else:
                        outs[s][f * 64 : (f + 1) * 64, here] = piece
        if mode == "both":
            outs[s][256:, :] = received[...]


def grads_half(pairs, width, mode, received=None):
    total = sum(right.shape[1] for _, right in pairs) // 2
    cores = 2 if mode == "both" else 1
    args = [v for lefts, right in pairs for v in (*(left for left, _ in lefts), right)]

    def kernel(*refs):
        given, at = [], 0
        for lefts, _ in pairs:
            count = len(lefts)
            skips = [skip for _, skip in lefts]
            given.append((list(zip(refs[at : at + count], skips)), refs[at + count]))
            at += count + 1
        rest = refs[at:]
        if mode == "other":
            rest = (rest[0], None, None, None, *rest[1:])
        grads_kernel(mode, width, given, *rest)

    out = call(
        kernel,
        {
            "other": (((4, 4, 64, total), BF16),),
            "own": (((4, 64, total), BF16),) * 4,
            "both": (((272, 2 * total), BF16),) * 4,
        }[mode],
        [SPACE_VMEM] * (len(args) + (mode != "other")),
        [pltpu.VMEM((cores * 512, 512), BF16), pltpu.VMEM((cores * 512, 2 * total), BF16)],
        (*args, *(() if mode == "other" else (received,))),
        flops=2 * 512 * 512 * total * 2,
        traffic=2**23,
        vmem=16,
    )
    return out[0] if mode == "other" else out


def second_sum(own, got):
    return sum(v.astype(F32) for v in (own, got[1], got[2], got[3]))


def scatter_first(parts, small=None):
    width = sum(p.shape[2] for p in parts)
    extra = [] if small is None else [split_rows(small, 64, 256)]
    last = {
        m: first_axis(jnp.concatenate([*(p[m].astype(BF16) for p in parts), *extra], axis=1), m)
        for m in (2, 1, 3)
    }
    came = sum(last[m].astype(F32) for m in (1, 2, 3))
    out, at = [], 0
    for p in parts:
        out.append(p[0] + came[:, at : at + p.shape[2]])
        at += p.shape[2]
    if small is None:
        return out
    return out, small + joined_rows(came[:, width:], small.shape)


def mixer_pull_kernel(*refs):
    blocks, proj, conv, wout = refs[:4], refs[4], refs[5], refs[6]
    d_conv, d_c, d_mixer = refs[7:]
    for m in range(4):
        d_mixer[m * 128 : (m + 1) * 128, :] = blocks[m][...]
    d_gated = jnp.dot(d_mixer[...], wout[...], preferred_element_type=F32)
    d_conv[...] = (d_gated * proj[:, 256:512]).astype(BF16)
    d_c[...] = (d_gated * conv[...]).astype(BF16)


def mixer_pull(blocks, proj, conv, wout):
    return call(
        mixer_pull_kernel,
        (((512, 256), BF16), ((512, 256), BF16)),
        [SPACE_VMEM] * 7,
        [pltpu.VMEM((512, 1024), BF16)],
        (*blocks, proj, conv, wout),
        flops=2 * 512 * 1024 * 256,
        traffic=2**21,
        vmem=8,
    )


def mixer_backward_kernel(*refs):
    blocks = refs[:4]
    d_conv, d_c, outside, proj, prod, scale, taps, length, win, gain_two = refs[4:14]
    sent = refs[14:18]
    d_proj, extra, small = refs[18:]
    _, _, _, z = position()
    small[...] = jnp.zeros((5, 1024), F32)
    sums = [0.0, 0.0, 0.0]
    for m in range(4):
        here = z ^ m
        rows = slice(m * 128, (m + 1) * 128)
        at = pl.multiple_of(((here + 1) % 4 ^ z) * 128, 128)
        inner = d_conv[pl.ds(at, 16), :].astype(F32)
        following = jnp.where(here < 3, inner, outside[...].astype(F32))
        places = first_token(m) + lax.broadcasted_iota(jnp.int32, (128, 256), 0)
        live = places < length[0, 0]
        one = jnp.where((places >= 1) & live, 1.0, 0.0)
        two = jnp.where((places >= 2) & live, 1.0, 0.0)
        one_back = jnp.where(places + 1 < length[0, 0], 1.0, 0.0)
        two_back = jnp.where(places + 2 < length[0, 0], 1.0, 0.0)
        pull = d_conv[rows, :].astype(F32)
        longer = jnp.concatenate([pull, following], axis=0)
        d_product = (
            taps[2:3, :] * pull
            + one_back * (taps[1:2, :] * longer[1:129])
            + two_back * (taps[0:1, :] * longer[2:130])
        )
        d_proj[rows, :256] = (d_product * proj[rows, 512:]).astype(BF16)
        d_proj[rows, 256:512] = d_c[rows, :]
        d_proj[rows, 512:] = (d_product * proj[rows, :256]).astype(BF16)
        sums[0] += jnp.sum(pull * two * prod[m, 14:142, :], axis=0, keepdims=True)
        sums[1] += jnp.sum(pull * one * prod[m, 15:143, :], axis=0, keepdims=True)
        sums[2] += jnp.sum(pull * prod[m, 16:, :], axis=0, keepdims=True)
    for h in range(2):
        lanes = pl.ds(pl.multiple_of((h * 4 + z) * 128, 128), 128)
        for i in range(3):
            small[2 + i : 3 + i, lanes] = sums[i][:, h * 128 : (h + 1) * 128]
    out = lax.dot_general(d_proj[...], win[...], CONTRACT_LAST, preferred_element_type=F32)
    gain = 0.0
    for m in range(4):
        rows = slice(m * 128, (m + 1) * 128)
        unit = blocks[m][:128, :].astype(F32) * scale[rows, :]
        gain += jnp.sum(out[rows] * unit, axis=0, keepdims=True)
        sent[m][...] = out[rows].astype(BF16)
    small[0:1, :] = gain
    small[1:2, :] = gain_two[...]
    high = small[...].astype(BF16)
    low = (small[...] - high.astype(F32)).astype(BF16)
    rows = jnp.concatenate([high.astype(F32), low.astype(F32), jnp.zeros((6, 1024), F32)], axis=0)
    extra[...] = rows.astype(BF16)


def mixer_backward(
    blocks, d_conv, d_c, outside, proj, prod, scale, taps, length, win, gain_two
):
    out = call(
        mixer_backward_kernel,
        (
            *[((128, 1024), BF16)] * 4,
            ((512, 768), BF16),
            ((16, 1024), BF16),
        ),
        [SPACE_VMEM] * 11 + [SPACE_SMEM] + [SPACE_VMEM] * 2,
        [pltpu.VMEM((5, 1024), F32)],
        (*blocks, d_conv, d_c, outside, proj, prod, scale, taps, length, win, gain_two),
        flops=2 * 512 * 1024 * 768,
        traffic=2**23,
    )
    return out[:4], out[4], out[5]


def body(tokens, lengths, gain_one, w_in, conv_weight, w_out, gain_two, w_gu, w_down, cotangent):
    z = lax.axis_index("z")
    tail = jnp.zeros((64, FF_PAD - FF_BLOCK), BF16)
    pack = jnp.concatenate(
        [w_in[:, 0], w_in[:, 1], w_in[:, 2], w_out.T]
        + [w_gu[0], tail, w_gu[1], tail, w_down.T, tail],
        axis=1,
    )
    first = all_first(pack)
    blocks = all_z(jnp.concatenate([tokens, cotangent], axis=0))
    mixer_mine = grouped_second(jnp.stack([v[:, :512] for v in first]))
    ends = jnp.stack([v[112:128] for v in blocks])
    behind = from_group(lax.dynamic_index_in_dim(ends, 3 ^ z, 0, keepdims=False), -1)
    mixer_mine, ffn_first = together(mixer_mine, jnp.stack([v[:, 512:] for v in first]))
    mixer_pieces = (mixer_mine, other_core(mixer_mine))
    ffn_got = {m: second_axis(ffn_first, m) for m in (1, 3)}
    behind, ffn_late = together(behind, ffn_first)
    ffn_got[2] = second_axis(ffn_late, 2)
    taps = jnp.concatenate(
        [
            lax.dynamic_slice_in_dim(conv_weight, z * 128, 128, 1),
            lax.dynamic_slice_in_dim(conv_weight, 512 + z * 128, 128, 1),
        ],
        axis=1,
    )
    residual = tokens.astype(F32)

    part, normed_one, proj, conv, prod, scale_one, gated, win, wout = mixer_forward(
        blocks, behind, gain_one[None], taps, lengths, mixer_pieces
    )
    middle = residual + sum_z(part)
    ffn_got, middle = together(ffn_got, middle)
    ffn_mine = [ffn_first, ffn_got[1], ffn_got[2], ffn_got[3]]
    scale_two = rms(middle)
    unit_two = middle * scale_two
    normed_own = (unit_two * gain_two).astype(BF16)
    ffn_pieces = both_cores(ffn_mine)
    normed_two = all_z(normed_own)

    d_two, d_gu, activation = ffn_block(
        normed_two, blocks, ffn_pieces
    )
    ffn_pairs = [
        ([(v, 0) for v in normed_two], d_gu),
        ([(v, 128) for v in blocks], activation),
    ]
    ffn_sent = grads_half(ffn_pairs, FF_PAD, "other")
    d_normed_two = sum_z(d_two)
    pulled = d_normed_two * gain_two
    d_middle = cotangent.astype(F32) + scale_two * (
        pulled - unit_two * jnp.mean(pulled * unit_two, axis=-1, keepdims=True)
    )
    gain_two_part = jnp.sum(d_normed_two * unit_two, axis=0)
    ffn_sent, d_mixer_own = together(ffn_sent, d_middle.astype(BF16))
    d_mixer_blocks = all_z(d_mixer_own)
    ffn_half = grads_half(ffn_pairs, FF_PAD, "own", other_core(ffn_sent))
    ffn_half, d_mixer_blocks = together(ffn_half, d_mixer_blocks)
    ffn_got = {m: second_axis(ffn_half[m], m) for m in (2, 1, 3)}

    d_conv, d_c = mixer_pull(d_mixer_blocks, proj, conv, wout)
    d_conv, act_late = together(d_conv, activation)
    outside = from_group(lax.dynamic_slice_in_dim(d_conv, z * 128, 16, 0), 1)
    ffn = down_projection(act_late, ffn_pieces)
    outside, ffn = together(outside, ffn)
    sent, d_projected, extra = mixer_backward(
        blocks, d_conv, d_c, outside, proj, prod, scale_one, taps, lengths, win,
        gain_two_part[None],
    )
    mixer_pairs = [
        ([(normed_one, 0)], d_projected),
        ([(v, 0) for v in d_mixer_blocks], gated),
    ]
    mixer_half = grads_half(mixer_pairs, 128, "both", extra)
    sent, mixer_half, ffn_got = together(sent, mixer_half, ffn_got)
    mixer_got = {m: second_axis(mixer_half[m], m) for m in (2, 1, 3)}
    d_normed_one = sum_z(sent)
    ffn, d_normed_one = together(ffn, d_normed_one)
    ffn_out = sum_z(ffn)
    mixed = (middle + ffn_out).astype(BF16)
    ffn_total = second_sum(ffn_half[0], ffn_got)
    mixer_total = second_sum(mixer_half[0], mixer_got)
    small = mixer_total[256:261] + mixer_total[261:266]
    (mixer_both, ffn_grads), small = scatter_first(
        [mixer_total[:256].reshape(4, 64, 1024), ffn_total], small
    )
    small = small + other_core(small)
    small = small + sum(along_z(small, m) for m in (2, 1, 3))
    mixer_grads = mixer_both[:, :512] + other_core(mixer_both[:, 512:].astype(BF16)).astype(F32)

    scale_own = rms(residual)
    unit_one = residual * scale_own
    pulled_one = d_normed_one * gain_one
    grad_tokens = d_middle + scale_own * (
        pulled_one - unit_one * jnp.mean(pulled_one * unit_one, axis=-1, keepdims=True)
    )

    return (
        mixed,
        grad_tokens,
        small[0],
        mixer_grads[:, :384].reshape(64, 3, 128),
        small[2:],
        mixer_grads[:, 384:].T,
        small[1],
        jnp.stack([ffn_grads[:, :FF_BLOCK], ffn_grads[:, FF_PAD : FF_PAD + FF_BLOCK]]),
        ffn_grads[:, 2 * FF_PAD : 2 * FF_PAD + FF_BLOCK].T,
    )


def solution(mesh):
    fine = Mesh(mesh.devices.reshape(SIZES), AXES)
    rows = P(AXES, None)
    fsdp_ctx = ("x", "core", "ylo")
    tp = ("yhi", "z")
    return jax.shard_map(
        body,
        mesh=fine,
        in_specs=(
            rows,
            P(("x", "core"), None),
            P(),
            P(fsdp_ctx, None, tp),
            P(),
            P(tp, fsdp_ctx),
            P(),
            P(None, fsdp_ctx, tp),
            P(tp, fsdp_ctx),
            rows,
        ),
        out_specs=(
            rows,
            rows,
            P(),
            P(fsdp_ctx, None, tp),
            P(),
            P(tp, fsdp_ctx),
            P(),
            P(None, fsdp_ctx, tp),
            P(tp, fsdp_ctx),
        ),
        check_vma=False,
    )
```
